256 devices in a mesh: row: 32 (over z, x_hi, core), col: 8 (over x_lo, y).
Axes of the slice: x: 4 (x_hi: 2, x_lo: 2; x = x_hi * 2 + x_lo), y: 4, z: 8, core: 2. Of those that a mesh axis runs over, the one named last changes fastest.
Arguments:
- queries: bfloat16 [16384, 4096], P(('row', 'col')), may hold values from -160 to 160
- keys: bfloat16 [16384, 512], P(('col', 'row')), may hold values from -6 to 6
- values: bfloat16 [16384, 512], P(('col', 'row')), may hold values from -6 to 6
- doc_lengths: int32 [16], replicated, may hold values from 1 to 8192, 16384 in all
Outputs:
- attended: bfloat16 [16384, 4096], P(('row', 'col'))
The draws below stay inside these ranges and needn't reach their ends.
Inputs may be any that keep to these rules, and one draw needn't show every extreme that they name: `doc_lengths`: the lengths sum to 16384; one document has exactly 8192 tokens.
All inputs are finite; a program needn't handle non-finite values.
Results may differ from the reference program's by a relative error of at most 0.015.
Values may be sent and summed in bfloat16 or wider, within the bound.
A program may use at most 256 MiB of HBM per device.

```python
import math
import jax
import jax.numpy as jnp
import numpy as np
from jax import lax

QUERY_HEADS = 32
KEY_VALUE_HEADS = 4
HEAD_SIZE = 128
QUERY_PER_KEY = 8
DOCS = 16
PACKED_TOKENS = 16384
MOST = 8192


def shared_keys(key):
    base_key = jax.random.fold_in(key, 11)
    drawn = jax.random.normal(base_key, (PACKED_TOKENS, KEY_VALUE_HEADS * HEAD_SIZE), jnp.float32)
    return jnp.clip(drawn, -6.0, 6.0)


def draw_keys(key, part):
    base_rows = shared_keys(key)
    result = base_rows
    return result.astype(jnp.bfloat16)


def draw_queries(key, part):
    key = jax.random.fold_in(key, 5)
    fresh = jnp.clip(jax.random.normal(jax.random.fold_in(key, 2), (PACKED_TOKENS, QUERY_HEADS * HEAD_SIZE), jnp.float32), -6.0, 6.0)
    result = fresh
    return result.astype(jnp.bfloat16)


def level_of(key, dims, pieces, smallest, high):
    def one(position, blocks):
        draws = jax.random.uniform(jax.random.fold_in(jax.random.fold_in(key, 6), position), (blocks,), jnp.float32, smallest / len(pieces), high / len(pieces))
        return jnp.repeat(jnp.exp(draws), dims[position] // blocks).reshape((-1,) + (1,) * (len(dims) - position - 1))

    loudness = one(*pieces[0])
    for cut in pieces[1:]:
        loudness = loudness * one(*cut)
    return loudness


def length_profile(amount, total, limit, lean):
    loads = [(1 << 20) // math.isqrt(rank ** lean) + 1 for rank in range(2, amount + 1)]
    spare, given = total - limit - (amount - 1), [1] * (amount - 1)
    while spare > 0:
        free = [i for i in range(amount - 1) if given[i] < limit]
        whole, remaining = sum([loads[i] for i in free]), spare
        for i in free:
            addition = min(limit - given[i], max(1, remaining * loads[i] // whole), spare)
            given[i] = given[i] + addition
            spare = spare - addition
    return np.array([limit] + given)


def ragged(rng, count, total, limit, slope):
    if count == 2:
        one = jax.random.randint(rng, (), max(1, total - limit), min(limit, total - 1) + 1)
        return jnp.stack([one, total - one])
    tallies = jnp.asarray(length_profile(count, total, limit, slope), jnp.int32)
    couples = (count - 1) // 2
    donor, receiver = tallies[1:1 + 2 * couples:2], tallies[2:2 + 2 * couples:2]
    room = jnp.minimum(donor - 1, limit - receiver)
    moved = jax.random.randint(jax.random.fold_in(rng, 1), (couples,), 0, 1 << 20) % (room + 1)
    tallies = tallies.at[1:1 + 2 * couples:2].set(donor - moved).at[2:2 + 2 * couples:2].set(receiver + moved)
    return tallies[jax.random.permutation(jax.random.fold_in(rng, 2), count)]


def noise(stream_key, extent, deviation, bound, pieces=(), kind=jnp.bfloat16):
    values = deviation * jax.random.normal(stream_key, extent, jnp.float32)
    if pieces:
        values = values * level_of(stream_key, extent, pieces, -0.22, 0.18)
    return jnp.clip(values, -bound, bound).astype(kind)


def setup_inputs(seed: int = 0) -> dict:
    key_of = jax.random.split(jax.random.key(seed), 5)
    return {
        "queries": draw_queries(jax.random.fold_in(key_of[4], 71), 0),
        "keys": draw_keys(jax.random.fold_in(key_of[4], 71), 0),
        "values": noise(key_of[2], (PACKED_TOKENS, KEY_VALUE_HEADS * HEAD_SIZE), 1.0, 6.0, ((0, 256),)),
        "doc_lengths": ragged(key_of[3], DOCS, PACKED_TOKENS, MOST, 2).astype(jnp.int32),
    }


def doc_of(positions, doc_ends):
    return jnp.sum((positions[:, None] >= doc_ends[None, :]).astype(jnp.int32), axis=1).astype(jnp.int32)


def reference(queries, keys, values, doc_lengths):
    doc_ends = jnp.cumsum(doc_lengths).astype(jnp.int32)
    key_pos = jnp.arange(PACKED_TOKENS, dtype=jnp.int32)
    key_doc = doc_of(key_pos, doc_ends)
    key_head_rows = keys.astype(jnp.float32).reshape(PACKED_TOKENS, KEY_VALUE_HEADS, HEAD_SIZE).transpose(1, 0, 2)
    value_head_rows = values.astype(jnp.float32).reshape(PACKED_TOKENS, KEY_VALUE_HEADS, HEAD_SIZE).transpose(1, 0, 2)
    scale = 1.0 / (HEAD_SIZE ** 0.5)
    window_extent = min(256, PACKED_TOKENS)
    count = PACKED_TOKENS // window_extent

    def one_block(index):
        start = (index * window_extent).astype(jnp.int32)
        query_row_slice = lax.dynamic_slice_in_dim(queries, start, window_extent, 0).astype(jnp.float32)
        query_head_rows = query_row_slice.reshape(window_extent, KEY_VALUE_HEADS, QUERY_PER_KEY, HEAD_SIZE).transpose(1, 0, 2, 3)
        query_pos = start + jnp.arange(window_extent, dtype=jnp.int32)
        query_doc = doc_of(query_pos, doc_ends)
        visible = (key_pos[None, :] <= query_pos[:, None]) & (key_doc[None, :] == query_doc[:, None])

        def one_head(inputs):
            q_head, k_head, v_head = inputs
            scores = jnp.einsum("qgd,kd->qgk", q_head, k_head) * scale
            masked = jnp.where(visible[:, None, :], scores, -jnp.inf)
            row_max = jnp.max(masked, axis=2)
            weights = jnp.where(visible[:, None, :], jnp.exp(scores - row_max[:, :, None]), 0.0)
            denominator = jnp.sum(weights, axis=2)
            rounded = weights.astype(jnp.bfloat16).astype(jnp.float32)
            numerator = jnp.einsum("qgk,kd->qgd", rounded, v_head)
            return numerator / denominator[:, :, None]

        result = lax.map(one_head, (query_head_rows, key_head_rows, value_head_rows))
        return result.transpose(1, 0, 2, 3).reshape(window_extent, QUERY_HEADS * HEAD_SIZE)

    blocks = lax.map(one_block, jnp.arange(count, dtype=jnp.int32))
    return blocks.reshape(PACKED_TOKENS, QUERY_HEADS * HEAD_SIZE).astype(jnp.bfloat16)
```

```python
import jax
import jax.numpy as jnp
from jax import lax
from jax.experimental import pallas as pl
from jax.experimental.pallas import tpu as pltpu
from jax.sharding import PartitionSpec as P

D = 128
G = 8
BF = jnp.bfloat16
F32 = jnp.float32
LOG2E = 1.4426950408889634
SCALE = LOG2E / D**0.5
HIDE = -1e30
FLOOR = -3e30
PIECE = 256
ROWS = 512
VR = 144
MESH = pl.DeviceIdType.MESH


def kernel(
    lengths,
    queries,
    keys,
    values,
    out,
    q_in,
    sub,
    kv,
    q_aug,
    kd,
    vt,
    acc,
    top,
    sb,
    mb,
    o_send,
    y_send,
    y_recv,
    x_send,
    x_recv,
    c_send,
    c_recv,
    o_ssem,
    o_rsem,
    l_sem,
):
    row = lax.axis_index("row")
    col = lax.axis_index("col")
    z = row // 4
    x_hi = (row // 2) % 2
    core = row % 2
    x_lo = col // 4
    y = col % 4
    x = x_hi * 2 + x_lo
    rank = x_hi * 4 + core * 2 + x_lo
    first = z * 2048 + rank * 256
    up = (lax.rem(row + 4, 32), col)
    down = (lax.rem(row + 28, 32), col)
    twin = (row + 1 - 2 * core, col)

    def at_y(d):
        return (row, x_lo * 4 + lax.rem(y + d, 4))

    def at_x(d, k):
        xd = lax.rem(x + d, 4)
        return (z * 4 + (xd // 2) * 2 + k, (xd % 2) * 4 + y)

    barrier = pltpu.get_barrier_semaphore()
    for d in (1, 2, 3):
        pl.semaphore_signal(barrier, inc=1, device_id=at_y(d), device_id_type=MESH)
    for d in (1, 2, 3):
        for k in (0, 1):
            pl.semaphore_signal(barrier, inc=1, device_id=at_x(d, k), device_id_type=MESH)
    for who in (twin, up, down):
        pl.semaphore_signal(barrier, inc=1, device_id=who, device_id_type=MESH)

    def cut(ref, head, width):
        return ref.at[:, pl.ds(pl.multiple_of(head * width, width), width)]

    def own_copies():
        return (
            pltpu.make_async_copy(cut(keys, y, D), sub.at[y, :, 0:D], l_sem.at[0]),
            pltpu.make_async_copy(cut(values, y, D), sub.at[y, :, D : 2 * D], l_sem.at[1]),
            pltpu.make_async_copy(cut(queries, y, G * D), q_in.at[y], l_sem.at[2]),
        )

    def y_copy(kind, d):
        head = lax.rem(y + d, 4)
        src, dst = (
            (cut(keys, head, D), sub.at[y, :, 0:D]),
            (cut(values, head, D), sub.at[y, :, D : 2 * D]),
            (cut(queries, head, G * D), q_in.at[y]),
        )[kind]
        return pltpu.make_async_remote_copy(
            src_ref=src,
            dst_ref=dst,
            send_sem=y_send.at[kind, d - 1],
            recv_sem=y_recv.at[kind, d - 1],
            device_id=at_y(d),
            device_id_type=MESH,
        )

    def y_wait(kind, d):
        peer = lax.rem(y + 4 - d, 4)
        dst = (sub.at[peer, :, 0:D], sub.at[peer, :, D : 2 * D], q_in.at[peer])[kind]
        pltpu.make_async_remote_copy(
            src_ref=dst,
            dst_ref=dst,
            send_sem=y_send.at[kind, d - 1],
            recv_sem=y_recv.at[kind, d - 1],
            device_id=at_y(d),
            device_id_type=MESH,
        ).wait_recv()

    for copy in own_copies():
        copy.start()

    acc[...] = jnp.zeros_like(acc)
    top[...] = jnp.full_like(top, FLOOR)
    vt[:, D:VR, :] = jnp.ones((2, VR - D, 4 * PIECE), BF)

    lane = lax.broadcasted_iota(jnp.int32, (1, D), 1)
    doc_first = jnp.zeros((1, D), jnp.int32)
    doc_end = jnp.zeros((1, D), jnp.int32)
    total = jnp.int32(0)
    for d in range(16):
        doc_first = jnp.where(lane == d, total, doc_first)
        total = total + lengths[d]
        doc_end = jnp.where(lane == d, total, doc_end)

    def in_doc(start, count):
        pos = start + lax.broadcasted_iota(jnp.int32, (count, D), 0)
        return (pos >= doc_first) & (pos < doc_end)

    pl.semaphore_wait(barrier, 12)
    for kind in (0, 1, 2):
        for d in (1, 3, 2):
            y_copy(kind, d).start()
    own = own_copies()
    own[0].wait()
    own[1].wait()
    for d in (1, 3, 2):
        y_wait(0, d)
        y_wait(1, d)

    def x_slot(chunk, who):
        rows = pl.ds(pl.multiple_of(who * 64, 64), 64)
        return kv.at[chunk * 8 + z, rows, :]

    def x_copy(d, j):
        chunk = x_lo * 4 + j
        return pltpu.make_async_remote_copy(
            src_ref=sub.at[j],
            dst_ref=x_slot(chunk, x_hi * 2 + core),
            send_sem=x_send.at[d, j],
            recv_sem=x_recv.at[chunk, x_hi * 2 + core],
            device_id=at_x(d, j % 2),
            device_id_type=MESH,
        )

    def x_local(j):
        chunk = x_lo * 4 + j
        return pltpu.make_async_copy(
            sub.at[j],
            x_slot(chunk, x_hi * 2 + core),
            x_recv.at[chunk, x_hi * 2 + core],
        )

    for j in range(4):

        @pl.when(core == j % 2)
        def _():
            x_local(j).start()

        @pl.when(core != j % 2)
        def _():
            x_copy(0, j).start()

        for d in (1, 3, 2):
            x_copy(d, j).start()

    own[2].wait()
    for d in (1, 3, 2):
        y_wait(2, d)

    for b in range(4):
        seen = in_doc(first + b * 64, 64)
        lanes = lax.broadcasted_iota(jnp.int32, (64, D), 1)
        wall = jnp.where(lanes < 16, jnp.where(seen, 0.0, HIDE), jnp.where(lanes == 16, HIDE, 0.0))
        wall = wall.astype(BF)
        for h in range(G):
            at = (b * G + h) * 64
            q_aug[at : at + 64, 0:D] = q_in[b, :, h * D : (h + 1) * D]
            q_aug[at : at + 64, D : 2 * D] = wall

    def route(chunk):
        last = jnp.minimum(chunk + 4, 7)
        before = jnp.where(chunk < 4, 1, 2)
        behind = jnp.maximum(chunk, 3) - before
        most_up = before + last - chunk
        most_down = behind + last - chunk
        u = lax.rem(z - chunk + before + 16, 8)
        v = lax.rem(last + behind - z + 16, 8)
        in_up = u <= most_up
        in_down = v <= most_down
        got_up = jnp.where(in_up, u, 0)
        got_down = jnp.where(in_down, v, 0)
        on_up = in_up & (u < most_up)
        on_down = in_down & (v < most_down)
        wanted = (z >= chunk) & (z <= chunk + 4)
        return got_up, got_down, on_up, on_down, wanted

    def source(got_up, got_down, i):
        both = jnp.minimum(got_up, got_down)
        paired = i <= 2 * both
        step = jnp.where(paired, (i + 1) // 2, i - both)
        rising = jnp.where(paired, lax.rem(i, 2) == 1, got_up > got_down)
        return lax.rem(jnp.where(rising, z - step, z + step) + 8, 8), rising

    def c_copy(way, piece):
        return pltpu.make_async_remote_copy(
            src_ref=kv.at[piece],
            dst_ref=kv.at[piece],
            send_sem=c_send.at[way, piece],
            recv_sem=c_recv.at[piece],
            device_id=(up, down, twin)[way],
            device_id_type=MESH,
        )

    def serve(i, act):
        def one(chunk, carry):
            got_up, got_down, on_up, on_down, wanted = route(chunk)
            src, rising = source(got_up, got_down, i)
            src = jnp.where(i == 0, z, src)
            piece = chunk * 8 + src
            mine = lax.rem(chunk, 2) == core
            there = i <= got_up + got_down
            go_up = mine & there & on_up & ((i == 0) | rising)
            go_down = mine & there & on_down & ((i == 0) | jnp.logical_not(rising))
            go_twin = mine & there & wanted
            if act:

                @pl.when(mine & (i == 0))
                def _():
                    for who in range(4):
                        pltpu.make_async_copy(
                            sub.at[0], x_slot(chunk, who), x_recv.at[chunk, who]
                        ).wait()

                @pl.when(there & ((mine & (i > 0)) | (jnp.logical_not(mine) & wanted)))
                def _():
                    c_copy(0, piece).wait_recv()

            for way, go in ((0, go_up), (1, go_down), (2, go_twin)):

                @pl.when(go)
                def _():
                    if act:
                        c_copy(way, piece).start()
                    else:
                        c_copy(way, piece).wait_send()

            return carry

        lax.fori_loop(0, 8, one, 0)

    def w_piece(step):
        src = lax.rem(z + step + 8, 8)
        chunk = jnp.where(src < rank, z, z - 4)
        live = chunk >= 0
        return jnp.where(live, chunk, z), jnp.where(live, src, z), live

    def pieces(i):
        got = []
        for back in (3, 2, 1):
            chunk = z - back
            live = chunk >= 0
            got_up, got_down, _, _, _ = route(jnp.maximum(chunk, 0))
            src, _ = source(got_up, got_down, i)
            src = jnp.where(i == 0, z, src)
            got.append((jnp.where(live, chunk, z), jnp.where(live, src, z), live))
        step = jnp.where(i == 1, -1, 0)
        step = jnp.where(i == 2, 1, step)
        step = jnp.where(i == 4, 2, step)
        step = jnp.where(i == 6, 4, step)
        step = jnp.where(i == 7, -3, step)
        chunk, src, live = w_piece(step)
        got.append((chunk, src, live & (i != 3) & (i != 5)))
        return got

    def ready(half, got):
        for n, (chunk, src, live) in enumerate(got):
            piece = chunk * 8 + src
            at = slice(n * PIECE, (n + 1) * PIECE)
            vt[half, 0:D, at] = kv[piece, :, D : 2 * D].T
            seen = in_doc(chunk * 2048 + src * 256, PIECE)
            lanes = lax.broadcasted_iota(jnp.int32, (PIECE, D), 1)
            flag = jnp.where(live, jnp.where(seen, 1.0, 0.0), jnp.where(lanes == 16, 1.0, 0.0))
            kd[at, :] = flag.astype(BF)

    def block(r):
        return pl.ds(pl.multiple_of(r * ROWS, ROWS), ROWS)

    def score(got, r, slot, diagonal=False):
        q = q_aug[block(r), :]
        best = None
        for n, (chunk, src, _) in enumerate(got):
            at = slice(n * PIECE, (n + 1) * PIECE)
            k = jnp.concatenate([kv[chunk * 8 + src, :, 0:D], kd[at, :]], axis=1)
            s = lax.dot_general(k, q, (((1,), (1,)), ((), ())), preferred_element_type=F32)
            if diagonal and n == len(got) - 1:
                key = lax.broadcasted_iota(jnp.int32, (PIECE, ROWS), 0)
                query = r * 64 + (lax.broadcasted_iota(jnp.int32, (PIECE, ROWS), 1) & 63)
                s = jnp.where(key <= query, s, HIDE)
            sb[slot, at, :] = s
            here = jnp.max(s, axis=0, keepdims=True)
            best = here if best is None else jnp.maximum(best, here)
        mb[slot, 0:1, :] = best

    def mix(half, count, r, slot):
        cols = block(r)
        old = top[0:1, cols]
        new = jnp.maximum(old, mb[slot, 0:1, :])
        shift = new * SCALE
        sums = acc[:, cols] * jnp.exp2((old - new) * SCALE)
        for n in range(count):
            at = slice(n * PIECE, (n + 1) * PIECE)
            w = jnp.exp2(sb[slot, at, :] * SCALE - shift).astype(BF)
            sums = sums + jnp.dot(vt[half, :, at], w, preferred_element_type=F32)
        acc[:, cols] = sums
        top[0:1, cols] = new

    serve(jnp.int32(0), True)
    start = pieces(jnp.int32(0))
    ready(0, start)
    score(start, 0, 0)

    def serve_for(i):
        low = jnp.where(i <= 5, i, i + 1)
        high = jnp.where(i < 5, i, i + 1)

        def one(j, carry):
            serve(j, True)
            return carry

        lax.fori_loop(low, high + 1, one, 0)

    def step(i, carry):
        half = lax.rem(i, 2)
        now = pieces(i)
        for r in range(3):
            score(now, r + 1, (r + 1) % 2)
            mix(half, 4, r, r % 2)
        serve_for(i + 1)
        later = pieces(i + 1)
        ready(1 - half, later)
        score(later, 0, 0)
        mix(half, 4, 3, 1)
        return carry

    lax.fori_loop(0, 7, step, 0)

    now = pieces(jnp.int32(7))
    for r in range(3):
        score(now, r + 1, (r + 1) % 2)
        mix(1, 4, r, r % 2)
    end = [w_piece(-2), w_piece(3), (z, rank, z >= 0)]
    ready(0, end)
    turn = [lax.rem(y + 1 + j, 4) for j in range(4)]
    score(end, turn[0], 0, True)
    mix(1, 4, 3, 1)

    def o_copy(d):
        who = lax.rem(y + d, 4)
        return pltpu.make_async_remote_copy(
            src_ref=o_send.at[who],
            dst_ref=cut(out, y, G * D),
            send_sem=o_ssem.at[d - 1],
            recv_sem=o_rsem.at[d - 1],
            device_id=at_y(d),
            device_id_type=MESH,
        )

    own_out = pltpu.make_async_copy(o_send.at[y], cut(out, y, G * D), l_sem.at[3])
    for j in range(4):
        if j < 3:
            score(end, turn[j + 1], (j + 1) % 2, True)
        mix(0, 3, turn[j], j % 2)
        cols = block(turn[j])
        o = (acc[0:D, cols] * (1.0 / acc[D : D + 1, cols])).T.astype(BF)
        for h in range(G):
            o_send[turn[j], :, h * D : (h + 1) * D] = o[h * 64 : (h + 1) * 64, :]
        if j < 3:
            o_copy(j + 1).start()
        else:
            own_out.start()

    for kind in (0, 1, 2):
        for d in (1, 3, 2):
            y_copy(kind, d).wait_send()
    for j in range(4):

        @pl.when(core != j % 2)
        def _():
            x_copy(0, j).wait_send()

        for d in (1, 3, 2):
            x_copy(d, j).wait_send()

    def drain(j, carry):
        serve(j, False)
        return carry

    lax.fori_loop(0, 8, drain, 0)
    for d in (1, 2, 3):
        o_copy(d).wait_send()
    for d in (1, 2, 3):
        peer = lax.rem(y + 4 - d, 4)
        pltpu.make_async_remote_copy(
            src_ref=o_send.at[peer],
            dst_ref=cut(out, peer, G * D),
            send_sem=o_ssem.at[d - 1],
            recv_sem=o_rsem.at[d - 1],
            device_id=at_y(d),
            device_id_type=MESH,
        ).wait_recv()
    own_out.wait()


def body(queries, keys, values, doc_lengths):
    anywhere = pl.BlockSpec(memory_space=pl.ANY)
    dma = pltpu.SemaphoreType.DMA
    return pl.pallas_call(
        kernel,
        out_shape=jax.ShapeDtypeStruct(queries.shape, BF),
        in_specs=[pl.BlockSpec(memory_space=pltpu.SMEM), anywhere, anywhere, anywhere],
        out_specs=anywhere,
        scratch_shapes=[
            pltpu.VMEM((4, 64, G * D), BF),
            pltpu.VMEM((4, 64, 2 * D), BF),
            pltpu.VMEM((64, PIECE, 2 * D), BF),
            pltpu.VMEM((4 * ROWS, 2 * D), BF),
            pltpu.VMEM((4 * PIECE, D), BF),
            pltpu.VMEM((2, VR, 4 * PIECE), BF),
            pltpu.VMEM((VR, 4 * ROWS), F32),
            pltpu.VMEM((8, 4 * ROWS), F32),
            pltpu.VMEM((2, 4 * PIECE, ROWS), F32),
            pltpu.VMEM((2, 8, ROWS), F32),
            pltpu.VMEM((4, 64, G * D), BF),
            dma((3, 3)),
            dma((3, 3)),
            dma((4, 4)),
            dma((8, 4)),
            dma((3, 64)),
            dma((64,)),
            dma((3,)),
            dma((3,)),
            dma((4,)),
        ],
        compiler_params=pltpu.CompilerParams(
            collective_id=0, has_side_effects=True, vmem_limit_bytes=48 * 2**20
        ),
        cost_estimate=pl.CostEstimate(
            flops=12 * 10**9, bytes_accessed=10**7, transcendentals=18 * 10**6
        ),
    )(doc_lengths, queries, keys, values)


def solution(mesh):
    return jax.shard_map(
        body,
        mesh=mesh,
        in_specs=(P(("row", "col"), None), P(("col", "row"), None), P(("col", "row"), None), P()),
        out_specs=P(("row", "col"), None),
        check_vma=False,
    )
```

```python
import jax
import jax.numpy as jnp
from jax import lax
from jax.experimental import pallas as pl
from jax.experimental.pallas import tpu as pltpu
from jax.sharding import PartitionSpec as P

D = 128
G = 8
BF = jnp.bfloat16
F32 = jnp.float32
LOG2E = 1.4426950408889634
SCALE = LOG2E / D**0.5
HIDE = -1e30
FLOOR = -3e30
PIECE = 256
ROWS = 512
VR = 144
MESH = pl.DeviceIdType.MESH


def kernel(
    lengths,
    queries,
    keys,
    values,
    out,
    q_in,
    sub,
    kv,
    q_aug,
    kd,
    vt,
    acc,
    top,
    sb,
    mb,
    o_send,
    y_send,
    y_recv,
    x_send,
    x_recv,
    c_send,
    t_send,
    c_recv,
    o_ssem,
    o_rsem,
    l_sem,
):
    row = lax.axis_index("row")
    col = lax.axis_index("col")
    z = row // 4
    x_hi = (row // 2) % 2
    core = row % 2
    x_lo = col // 4
    y = col % 4
    x = x_hi * 2 + x_lo
    rank = x_hi * 4 + core * 2 + x_lo
    first = z * 2048 + rank * 256
    up = (lax.rem(row + 4, 32), col)
    down = (lax.rem(row + 28, 32), col)
    twin = (row + 1 - 2 * core, col)

    def at_y(d):
        return (row, x_lo * 4 + lax.rem(y + d, 4))

    def at_x(d, k):
        xd = lax.rem(x + d, 4)
        return (z * 4 + (xd // 2) * 2 + k, (xd % 2) * 4 + y)

    barrier = pltpu.get_barrier_semaphore()
    for d in (1, 2, 3):
        pl.semaphore_signal(barrier, inc=1, device_id=at_y(d), device_id_type=MESH)
    for d in (1, 2, 3):
        for k in (0, 1):
            pl.semaphore_signal(barrier, inc=1, device_id=at_x(d, k), device_id_type=MESH)
    for who in (twin, up, down):
        pl.semaphore_signal(barrier, inc=1, device_id=who, device_id_type=MESH)

    def cut(ref, head, width):
        return ref.at[:, pl.ds(pl.multiple_of(head * width, width), width)]

    def own_copies():
        return (
            pltpu.make_async_copy(cut(keys, y, D), sub.at[y, :, 0:D], l_sem.at[0]),
            pltpu.make_async_copy(cut(values, y, D), sub.at[y, :, D : 2 * D], l_sem.at[1]),
            pltpu.make_async_copy(cut(queries, y, G * D), q_in.at[y], l_sem.at[2]),
        )

    def y_copy(kind, d):
        head = lax.rem(y + d, 4)
        src, dst = (
            (cut(keys, head, D), sub.at[y, :, 0:D]),
            (cut(values, head, D), sub.at[y, :, D : 2 * D]),
            (cut(queries, head, G * D), q_in.at[y]),
        )[kind]
        return pltpu.make_async_remote_copy(
            src_ref=src,
            dst_ref=dst,
            send_sem=y_send.at[kind, d - 1],
            recv_sem=y_recv.at[kind, d - 1],
            device_id=at_y(d),
            device_id_type=MESH,
        )

    def y_wait(kind, d):
        peer = lax.rem(y + 4 - d, 4)
        dst = (sub.at[peer, :, 0:D], sub.at[peer, :, D : 2 * D], q_in.at[peer])[kind]
        pltpu.make_async_remote_copy(
            src_ref=dst,
            dst_ref=dst,
            send_sem=y_send.at[kind, d - 1],
            recv_sem=y_recv.at[kind, d - 1],
            device_id=at_y(d),
            device_id_type=MESH,
        ).wait_recv()

    for copy in own_copies():
        copy.start()

    acc[...] = jnp.zeros_like(acc)
    top[...] = jnp.full_like(top, FLOOR)
    vt[:, D:VR, :] = jnp.ones((2, VR - D, 4 * PIECE), BF)

    lane = lax.broadcasted_iota(jnp.int32, (1, D), 1)
    doc_first = jnp.zeros((1, D), jnp.int32)
    doc_end = jnp.zeros((1, D), jnp.int32)
    total = jnp.int32(0)
    for d in range(16):
        doc_first = jnp.where(lane == d, total, doc_first)
        total = total + lengths[d]
        doc_end = jnp.where(lane == d, total, doc_end)

    def in_doc(offsets, start):
        pos = start + offsets
        return (pos >= doc_first) & (pos < doc_end)

    def spread(i):
        return (i & 63) + ((i >> 6) & 1) * 128 + ((i >> 7) & 1) * 64

    pl.semaphore_wait(barrier, 12)
    for kind in (0, 1, 2):
        for d in (1, 3, 2):
            y_copy(kind, d).start()
    own = own_copies()
    own[0].wait()
    own[1].wait()
    for d in (1, 3, 2):
        y_wait(0, d)
        y_wait(1, d)

    def x_slot(chunk, half, who):
        return kv.at[chunk * 8 + z, half, pl.ds(pl.multiple_of(who * 64, 64), 64), :]

    def x_copy(n, j):
        chunk = x_lo * 4 + j
        return pltpu.make_async_remote_copy(
            src_ref=sub.at[j],
            dst_ref=x_slot(chunk, core, x_hi),
            send_sem=x_send.at[n, j],
            recv_sem=x_recv.at[chunk, x_hi],
            device_id=at_x(lax.rem(x_lo + core, 2) + 2 * n, j % 2),
            device_id_type=MESH,
        )

    def x_local(j):
        chunk = x_lo * 4 + j
        return pltpu.make_async_copy(
            sub.at[j], x_slot(chunk, core, x_hi), x_recv.at[chunk, x_hi]
        )

    for j in range(4):
        stays = (x_lo == core) & (core == j % 2)

        @pl.when(stays)
        def _():
            x_local(j).start()

        @pl.when(jnp.logical_not(stays))
        def _():
            x_copy(0, j).start()

        x_copy(1, j).start()

    own[2].wait()
    for d in (1, 3, 2):
        y_wait(2, d)

    for b in range(4):
        seen = in_doc(lax.broadcasted_iota(jnp.int32, (64, D), 0), first + b * 64)
        lanes = lax.broadcasted_iota(jnp.int32, (64, D), 1)
        wall = jnp.where(lanes < 16, jnp.where(seen, 0.0, HIDE), jnp.where(lanes == 16, HIDE, 0.0))
        wall = wall.astype(BF)
        for h in range(G):
            at = (b * G + h) * 64
            q_aug[at : at + 64, 0:D] = q_in[b, :, h * D : (h + 1) * D]
            q_aug[at : at + 64, D : 2 * D] = wall

    def route(chunk):
        last = jnp.minimum(chunk + 4, 7)
        before = 1 + lax.rem(chunk, 2)
        behind = jnp.maximum(chunk, 3) - before
        most_up = before + last - chunk
        most_down = behind + last - chunk
        u = lax.rem(z - chunk + before + 16, 8)
        v = lax.rem(last + behind - z + 16, 8)
        in_up = u <= most_up
        in_down = v <= most_down
        got_up = jnp.where(in_up, u, 0)
        got_down = jnp.where(in_down, v, 0)
        on_up = in_up & (u < most_up)
        on_down = in_down & (v < most_down)
        wanted = (z >= chunk) & (z <= chunk + 4)
        return got_up, got_down, on_up, on_down, wanted

    def source(got_up, got_down, i):
        both = jnp.minimum(got_up, got_down)
        paired = i <= 2 * both
        step = jnp.where(paired, (i + 1) // 2, i - both)
        rising = jnp.where(paired, lax.rem(i, 2) == 1, got_up > got_down)
        return lax.rem(jnp.where(rising, z - step, z + step) + 8, 8)

    def c_copy(way, half, piece, side=0):
        who = (up, down, at_x(1 + 2 * side, core), twin)[way]
        return pltpu.make_async_remote_copy(
            src_ref=kv.at[piece, half],
            dst_ref=kv.at[piece, half],
            send_sem=t_send.at[half, piece] if way == 3 else c_send.at[way, piece],
            recv_sem=c_recv.at[half, piece],
            device_id=who,
            device_id_type=MESH,
        )

    def pass_on(act, chunk, src, ways):
        piece = chunk * 8 + src
        side = lax.rem(chunk // 2 + src, 2)
        for way, go in enumerate(ways):

            @pl.when(go)
            def _():
                copy = c_copy(way, x_lo, piece, side)
                if act:
                    copy.start()
                else:
                    copy.wait_send()

    def four(first_chunk, one):
        def each(j, carry):
            one(first_chunk + 2 * j)
            return carry

        lax.fori_loop(0, 4, each, 0)

    def sides(t, got_up, got_down):
        return (
            (t <= got_up, lax.rem(z - t + 8, 8)),
            (t <= got_down, lax.rem(z + t, 8)),
        )

    def chain_first(act):
        def one(chunk):
            _, _, on_up, on_down, wanted = route(chunk)
            if act:
                for who in range(2):
                    pltpu.make_async_copy(
                        sub.at[0], x_slot(chunk, x_lo, who), x_recv.at[chunk, who]
                    ).wait()
            pass_on(act, chunk, z, (on_up, on_down, wanted, wanted))

        four(core, one)

    def chain(t, act):
        def one(chunk):
            got_up, got_down, on_up, on_down, wanted = route(chunk)
            up_side, down_side = sides(t, got_up, got_down)
            for (there, src), ways in (
                (up_side, (on_up, None)),
                (down_side, (None, on_down)),
            ):

                @pl.when(there)
                def _():
                    if act:
                        c_copy(3, x_lo, chunk * 8 + src).wait_recv()
                    never = chunk < 0
                    pass_on(
                        act,
                        chunk,
                        src,
                        tuple(never if w is None else w for w in ways) + (wanted, wanted),
                    )

        four(core, one)

    def across(t, act):
        def one(chunk):
            got_up, got_down, _, _, wanted = route(chunk)
            for there, src in sides(t, got_up, got_down):

                @pl.when(there & wanted)
                def _():
                    copy = c_copy(3, 1 - x_lo, chunk * 8 + src)
                    if act:
                        copy.wait_recv()
                        copy.start()
                    else:
                        copy.wait_send()

        four(core, one)

    def across_first(act):
        def one(chunk):
            wanted = route(chunk)[4]

            @pl.when(wanted)
            def _():
                copy = c_copy(3, 1 - x_lo, chunk * 8 + z)
                if act:
                    copy.wait_recv()
                    copy.start()
                else:
                    copy.wait_send()

        four(core, one)

    def from_twin(t):
        def one(chunk):
            got_up, got_down, _, _, wanted = route(chunk)
            for there, src in sides(t, got_up, got_down):

                @pl.when(there & wanted)
                def _():
                    for half in range(2):
                        c_copy(3, half, chunk * 8 + src).wait_recv()

        four(1 - core, one)

    def from_twin_first():
        def one(chunk):
            wanted = route(chunk)[4]

            @pl.when(wanted)
            def _():
                for half in range(2):
                    c_copy(3, half, chunk * 8 + z).wait_recv()

        four(1 - core, one)

    def w_piece(step):
        src = lax.rem(z + step + 8, 8)
        chunk = jnp.where(src < rank, z, z - 4)
        live = chunk >= 0
        return jnp.where(live, chunk, z), jnp.where(live, src, z), live

    near = jnp.where(lax.rem(z, 2) == 0, 2, -2)

    def pieces(i):
        got = []
        for back in (3, 2, 1):
            chunk = z - back
            live = chunk >= 0
            got_up, got_down, _, _, _ = route(jnp.maximum(chunk, 0))
            src = jnp.where(i == 0, z, source(got_up, got_down, i))
            got.append((jnp.where(live, chunk, z), jnp.where(live, src, z), live))
        step = jnp.where(i == 1, -1, 0)
        for at, value in ((2, 1), (3, near), (4, 4), (5, 3), (6, -3), (7, -near)):
            step = jnp.where(i == at, value, step)
        got.append(w_piece(step))
        return got

    def ready(half, got):
        for n, (chunk, src, live) in enumerate(got):
            piece = chunk * 8 + src
            at = slice(n * PIECE, (n + 1) * PIECE)
            vt[half, 0:D, at] = kv[piece, :, :, D : 2 * D].reshape(PIECE, D).T
            seen = in_doc(spread(lax.broadcasted_iota(jnp.int32, (PIECE, D), 0)), chunk * 2048 + src * 256)
            lanes = lax.broadcasted_iota(jnp.int32, (PIECE, D), 1)
            flag = jnp.where(live, jnp.where(seen, 1.0, 0.0), jnp.where(lanes == 16, 1.0, 0.0))
            kd[half, at, :] = flag.astype(BF)

    turn = [lax.rem(y + 1 + j, 4) for j in range(4)]

    def block(r):
        return pl.ds(pl.multiple_of(r * ROWS, ROWS), ROWS)

    def score(half, got, r, slot, diagonal=False):
        q = q_aug[block(r), :]
        best = None
        for n, (chunk, src, _) in enumerate(got):
            at = slice(n * PIECE, (n + 1) * PIECE)
            k = kv[chunk * 8 + src, :, :, 0:D].reshape(PIECE, D)
            k = jnp.concatenate([k, kd[half, at, :]], axis=1)
            s = lax.dot_general(k, q, (((1,), (1,)), ((), ())), preferred_element_type=F32)
            if diagonal:
                key = spread(lax.broadcasted_iota(jnp.int32, (PIECE, ROWS), 0))
                query = r * 64 + (lax.broadcasted_iota(jnp.int32, (PIECE, ROWS), 1) & 63)
                s = jnp.where(key <= query, s, HIDE)
            sb[slot, at, :] = s
            here = jnp.max(s, axis=0, keepdims=True)
            best = here if best is None else jnp.maximum(best, here)
        mb[slot, 0:1, :] = best

    def mix(half, count, r, slot):
        cols = block(r)
        old = top[0:1, cols]
        new = jnp.maximum(old, mb[slot, 0:1, :])
        shift = new * SCALE
        sums = acc[:, cols] * jnp.exp2((old - new) * SCALE)
        for n in range(count):
            at = slice(n * PIECE, (n + 1) * PIECE)
            w = jnp.exp2(sb[slot, at, :] * SCALE - shift).astype(BF)
            sums = sums + jnp.dot(vt[half, :, at], w, preferred_element_type=F32)
        acc[:, cols] = sums
        top[0:1, cols] = new

    chain_first(True)
    chain(jnp.int32(1), True)
    across_first(True)
    from_twin_first()
    start = pieces(jnp.int32(0))
    ready(0, start)
    score(0, start, turn[0], 0)

    def step(i, carry):
        half = lax.rem(i, 2)
        now = pieces(i)
        score(half, now, turn[1], 1)
        mix(half, 4, turn[0], 0)
        score(half, now, turn[2], 0)
        mix(half, 4, turn[1], 1)
        chain(i + 2, True)
        across(i + 1, True)
        score(half, now, turn[3], 1)
        mix(half, 4, turn[2], 0)
        from_twin(i + 1)
        later = pieces(i + 1)
        ready(1 - half, later)
        score(1 - half, later, turn[0], 0)
        mix(half, 4, turn[3], 1)
        return carry

    lax.fori_loop(0, 7, step, 0)

    now = pieces(jnp.int32(7))
    end = [(z, rank, z >= 0)]
    ready(0, end)

    def o_copy(d):
        who = lax.rem(y + d, 4)
        return pltpu.make_async_remote_copy(
            src_ref=o_send.at[who],
            dst_ref=cut(out, y, G * D),
            send_sem=o_ssem.at[d - 1],
            recv_sem=o_rsem.at[d - 1],
            device_id=at_y(d),
            device_id_type=MESH,
        )

    own_out = pltpu.make_async_copy(o_send.at[y], cut(out, y, G * D), l_sem.at[3])
    for j in range(4):
        score(0, end, turn[j], 1, True)
        mix(1, 4, turn[j], 0)
        if j < 3:
            score(1, now, turn[j + 1], 0)
        mix(0, 1, turn[j], 1)
        cols = block(turn[j])
        o = (acc[0:D, cols] * (1.0 / acc[D : D + 1, cols])).T.astype(BF)
        for h in range(G):
            o_send[turn[j], :, h * D : (h + 1) * D] = o[h * 64 : (h + 1) * 64, :]
        if j < 3:
            o_copy(j + 1).start()
        else:
            own_out.start()

    for kind in (0, 1, 2):
        for d in (1, 3, 2):
            y_copy(kind, d).wait_send()
    for j in range(4):

        @pl.when(jnp.logical_not((x_lo == core) & (core == j % 2)))
        def _():
            x_copy(0, j).wait_send()

        x_copy(1, j).wait_send()

    chain_first(False)
    across_first(False)

    def drain(t, carry):
        chain(t, False)
        across(t, False)
        return carry

    lax.fori_loop(1, 7, drain, 0)
    for d in (1, 2, 3):
        o_copy(d).wait_send()
    for d in (1, 2, 3):
        peer = lax.rem(y + 4 - d, 4)
        pltpu.make_async_remote_copy(
            src_ref=o_send.at[peer],
            dst_ref=cut(out, peer, G * D),
            send_sem=o_ssem.at[d - 1],
            recv_sem=o_rsem.at[d - 1],
            device_id=at_y(d),
            device_id_type=MESH,
        ).wait_recv()
    own_out.wait()


def body(queries, keys, values, doc_lengths):
    anywhere = pl.BlockSpec(memory_space=pl.ANY)
    hbm = pl.BlockSpec(memory_space=pltpu.HBM)
    dma = pltpu.SemaphoreType.DMA
    return pl.pallas_call(
        kernel,
        out_shape=jax.ShapeDtypeStruct(queries.shape, BF),
        in_specs=[pl.BlockSpec(memory_space=pltpu.SMEM), hbm, hbm, hbm],
        out_specs=anywhere,
        scratch_shapes=[
            pltpu.VMEM((4, 64, G * D), BF),
            pltpu.VMEM((4, 64, 2 * D), BF),
            pltpu.VMEM((64, 2, PIECE // 2, 2 * D), BF),
            pltpu.VMEM((4 * ROWS, 2 * D), BF),
            pltpu.VMEM((2, 4 * PIECE, D), BF),
            pltpu.VMEM((2, VR, 4 * PIECE), BF),
            pltpu.VMEM((VR, 4 * ROWS), F32),
            pltpu.VMEM((8, 4 * ROWS), F32),
            pltpu.VMEM((2, 4 * PIECE, ROWS), F32),
            pltpu.VMEM((2, 8, ROWS), F32),
            pltpu.VMEM((4, 64, G * D), BF),
            dma((3, 3)),
            dma((3, 3)),
            dma((2, 4)),
            dma((8, 2)),
            dma((3, 64)),
            dma((2, 64)),
            dma((2, 64)),
            dma((3,)),
            dma((3,)),
            dma((4,)),
        ],
        compiler_params=pltpu.CompilerParams(
            collective_id=0, has_side_effects=True, vmem_limit_bytes=60 * 2**20
        ),
        cost_estimate=pl.CostEstimate(
            flops=12 * 10**9, bytes_accessed=10**7, transcendentals=18 * 10**6
        ),
    )(doc_lengths, queries, keys, values)


def solution(mesh):
    return jax.shard_map(
        body,
        mesh=mesh,
        in_specs=(P(("row", "col"), None), P(("col", "row"), None), P(("col", "row"), None), P()),
        out_specs=P(("row", "col"), None),
        check_vma=False,
    )
```

```python
import jax
import jax.numpy as jnp
from jax import lax
from jax.experimental import pallas as pl
from jax.experimental.pallas import tpu as pltpu
from jax.sharding import PartitionSpec as P

D = 128
G = 8
BF = jnp.bfloat16
F32 = jnp.float32
LOG2E = 1.4426950408889634
SCALE = LOG2E / D**0.5
HIDE = -1e30
FLOOR = -3e30
PIECE = 256
ROWS = 512
VR = 144
MESH = pl.DeviceIdType.MESH


def kernel(
    lengths,
    queries,
    keys,
    values,
    out,
    q_in,
    kv,
    q_aug,
    kd,
    vt,
    acc,
    top,
    sb,
    mb,
    o_send,
    k_send,
    k_recv,
    q_send,
    q_recv,
    c_send,
    c_recv,
    x_recv,
    t_send,
    t_recv,
    o_ssem,
    o_rsem,
    l_sem,
):
    row = lax.axis_index("row")
    col = lax.axis_index("col")
    z = row // 4
    x_hi = (row // 2) % 2
    core = row % 2
    x_lo = col // 4
    y = col % 4
    x = x_hi * 2 + x_lo
    rank = x_hi * 4 + core * 2 + x_lo
    first = z * 2048 + rank * 256
    up = (lax.rem(row + 4, 32), col)
    down = (lax.rem(row + 28, 32), col)
    twin = (row + 1 - 2 * core, col)

    def at_y(d):
        return (row, x_lo * 4 + lax.rem(y + d, 4))

    def at_x(d, k):
        xd = lax.rem(x + d, 4)
        return (z * 4 + (xd // 2) * 2 + k, (xd % 2) * 4 + y)

    selfish = (lax.rem(y, 2) == core) & (core == x_lo)

    barrier = pltpu.get_barrier_semaphore()

    def greet(who):
        pl.semaphore_signal(barrier, inc=1, device_id=who, device_id_type=MESH)

    for who in (twin, up, down, at_x(1, core), at_x(3, core), at_y(1), at_y(2), at_y(3)):
        greet(who)
    for j in range(4):
        chunk = core + 2 * j
        for n in range(2):
            who = (z * 4 + n * 2 + x_lo, chunk)

            @pl.when(jnp.logical_not(selfish & (n == x_hi) & (chunk == col)))
            def _():
                greet(who)

    def cut(ref, head, width):
        return ref.at[:, pl.ds(pl.multiple_of(head * width, width), width)]

    def slot(kind, chunk, half, who):
        rows = pl.ds(pl.multiple_of(who * 64, 64), 64)
        return kv.at[chunk * 8 + z, half, rows, kind * D : (kind + 1) * D]

    def k_copy(kind, n, d):
        head = lax.rem(y + d, 4)
        return pltpu.make_async_remote_copy(
            src_ref=cut((keys, values)[kind], head, D),
            dst_ref=slot(kind, col, core, x_hi),
            send_sem=k_send.at[kind, n, d],
            recv_sem=k_recv.at[kind, col, x_hi],
            device_id=(z * 4 + n * 2 + lax.rem(y, 2), core * 4 + head),
            device_id_type=MESH,
        )

    def k_local(kind):
        return pltpu.make_async_copy(
            cut((keys, values)[kind], y, D),
            slot(kind, col, core, x_hi),
            k_recv.at[kind, col, x_hi],
        )

    def k_each(act):
        for d in (1, 3, 2, 0):
            for n in range(2):

                def one():
                    for kind in range(2):
                        copy = k_copy(kind, n, d)
                        if act:
                            copy.start()
                        else:
                            copy.wait_send()

                if d == 0:
                    pl.when(jnp.logical_not(selfish & (n == x_hi)))(one)
                else:
                    one()

    own_q = pltpu.make_async_copy(cut(queries, y, G * D), q_in.at[y], l_sem.at[0])

    def q_copy(d):
        return pltpu.make_async_remote_copy(
            src_ref=cut(queries, lax.rem(y + d, 4), G * D),
            dst_ref=q_in.at[y],
            send_sem=q_send.at[d - 1],
            recv_sem=q_recv.at[d - 1],
            device_id=at_y(d),
            device_id_type=MESH,
        )

    def q_wait(d):
        dst = q_in.at[lax.rem(y + 4 - d, 4)]
        pltpu.make_async_remote_copy(
            src_ref=dst,
            dst_ref=dst,
            send_sem=q_send.at[d - 1],
            recv_sem=q_recv.at[d - 1],
            device_id=at_y(d),
            device_id_type=MESH,
        ).wait_recv()

    own_q.start()

    @pl.when(selfish)
    def _():
        for kind in range(2):
            k_local(kind).start()

    acc[...] = jnp.zeros_like(acc)
    top[...] = jnp.full_like(top, FLOOR)
    vt[:, D:VR, :] = jnp.ones((2, VR - D, 5 * PIECE), BF)

    lane = lax.broadcasted_iota(jnp.int32, (1, D), 1)
    doc_first = jnp.zeros((1, D), jnp.int32)
    doc_end = jnp.zeros((1, D), jnp.int32)
    total = jnp.int32(0)
    for d in range(16):
        doc_first = jnp.where(lane == d, total, doc_first)
        total = total + lengths[d]
        doc_end = jnp.where(lane == d, total, doc_end)

    def in_doc(offsets, start):
        pos = start + offsets
        return (pos >= doc_first) & (pos < doc_end)

    def spread(i):
        return (i & 63) + ((i >> 6) & 1) * 128 + ((i >> 7) & 1) * 64

    pl.semaphore_wait(barrier, 16 - jnp.where(selfish, 1, 0))
    k_each(True)
    for d in (1, 3, 2):
        q_copy(d).start()

    def build(b):
        offsets = lax.broadcasted_iota(jnp.int32, (64, D), 0)
        seen = in_doc(offsets, first + b * 64)
        lanes = lax.broadcasted_iota(jnp.int32, (64, D), 1)
        wall = jnp.where(lanes < 16, jnp.where(seen, 0.0, HIDE), jnp.where(lanes == 16, HIDE, 0.0))
        wall = wall.astype(BF)
        for h in range(G):
            at = pl.ds(pl.multiple_of((b * G + h) * 64, 64), 64)
            q_aug[at, 0:D] = q_in[b, :, h * D : (h + 1) * D]
            q_aug[at, D : 2 * D] = wall

    def route(chunk):
        last = jnp.minimum(chunk + 4, 7)
        before = 1 + lax.rem(chunk, 2)
        behind = jnp.maximum(chunk, 3) - before
        most_up = before + last - chunk
        most_down = behind + last - chunk
        u = lax.rem(z - chunk + before + 16, 8)
        v = lax.rem(last + behind - z + 16, 8)
        in_up = u <= most_up
        in_down = v <= most_down
        got_up = jnp.where(in_up, u, 0)
        got_down = jnp.where(in_down, v, 0)
        on_up = in_up & (u < most_up)
        on_down = in_down & (v < most_down)
        wanted = (z >= chunk) & (z <= chunk + 4)
        return got_up, got_down, on_up, on_down, wanted

    def source(got_up, got_down, i):
        both = jnp.minimum(got_up, got_down)
        paired = i <= 2 * both
        step = jnp.where(paired, (i + 1) // 2, i - both)
        rising = jnp.where(paired, lax.rem(i, 2) == 1, got_up > got_down)
        return lax.rem(jnp.where(rising, z - step, z + step) + 8, 8)

    mine = [(core + 2 * j, route(core + 2 * j)) for j in range(4)]
    theirs = [(1 - core + 2 * j, route(1 - core + 2 * j)) for j in range(4)]

    def c_copy(way, piece, side=0):
        who = (up, down, at_x(1 + 2 * side, core))[way]
        return pltpu.make_async_remote_copy(
            src_ref=kv.at[piece, x_lo],
            dst_ref=kv.at[piece, x_lo],
            send_sem=c_send.at[way, piece],
            recv_sem=c_recv.at[piece],
            device_id=who,
            device_id_type=MESH,
        )

    def x_arrival(piece):
        return pltpu.make_async_remote_copy(
            src_ref=kv.at[piece, 1 - x_lo],
            dst_ref=kv.at[piece, 1 - x_lo],
            send_sem=c_send.at[2, piece],
            recv_sem=x_recv.at[piece],
            device_id=up,
            device_id_type=MESH,
        )

    def x_copy(piece, side):
        return pltpu.make_async_remote_copy(
            src_ref=kv.at[piece, x_lo],
            dst_ref=kv.at[piece, x_lo],
            send_sem=c_send.at[2, piece],
            recv_sem=x_recv.at[piece],
            device_id=at_x(1 + 2 * side, core),
            device_id_type=MESH,
        )

    def t_copy(piece):
        return pltpu.make_async_remote_copy(
            src_ref=kv.at[piece],
            dst_ref=kv.at[piece],
            send_sem=t_send.at[piece],
            recv_sem=t_recv.at[piece],
            device_id=twin,
            device_id_type=MESH,
        )

    def do(act, copy):
        if act:
            copy.start()
        else:
            copy.wait_send()

    def spread_x(act, chunk, src):
        do(act, x_copy(chunk * 8 + src, lax.rem(chunk // 2 + src, 2)))

    def sides(t, got_up, got_down):
        return (
            (t <= got_up, lax.rem(z - t + 8, 8)),
            (t <= got_down, lax.rem(z + t, 8)),
        )

    def chain_first(act):
        for chunk, (_, _, on_up, on_down, wanted) in mine:
            if act:
                for who in range(2):
                    for kind in range(2):
                        pltpu.make_async_copy(
                            slot(kind, chunk, x_lo, who),
                            slot(kind, chunk, x_lo, who),
                            k_recv.at[kind, chunk, who],
                        ).wait()
            piece = chunk * 8 + z

            @pl.when(on_up)
            def _():
                do(act, c_copy(0, piece))

            @pl.when(on_down)
            def _():
                do(act, c_copy(1, piece))

            @pl.when(wanted)
            def _():
                spread_x(act, chunk, z)

    def chain(t, act):
        for chunk, (got_up, got_down, on_up, on_down, wanted) in mine:
            for way, (there, src) in enumerate(sides(t, got_up, got_down)):

                @pl.when(there)
                def _():
                    piece = chunk * 8 + src
                    if act:
                        c_copy(way, piece).wait_recv()

                    @pl.when((on_up, on_down)[way])
                    def _():
                        do(act, c_copy(way, piece))

                    @pl.when(wanted)
                    def _():
                        spread_x(act, chunk, src)

    def across(t, act):
        for chunk, (got_up, got_down, _, _, wanted) in mine:
            for there, src in sides(t, got_up, got_down):

                @pl.when(there & wanted)
                def _():
                    piece = chunk * 8 + src
                    if act:
                        x_arrival(piece).wait_recv()
                    do(act, t_copy(piece))

    def across_first(act):
        for chunk, route_of in mine:

            @pl.when(route_of[4])
            def _():
                piece = chunk * 8 + z
                if act:
                    x_arrival(piece).wait_recv()
                do(act, t_copy(piece))

    def from_twin(t):
        for chunk, (got_up, got_down, _, _, wanted) in theirs:
            for there, src in sides(t, got_up, got_down):

                @pl.when(there & wanted)
                def _():
                    t_copy(chunk * 8 + src).wait_recv()

    def from_twin_first():
        for chunk, route_of in theirs:

            @pl.when(route_of[4])
            def _():
                t_copy(chunk * 8 + z).wait_recv()

    def w_piece(step):
        src = lax.rem(z + step + 8, 8)
        chunk = jnp.where(src < rank, z, z - 4)
        live = chunk >= 0
        return jnp.where(live, chunk, z), jnp.where(live, src, z), live

    near = jnp.where(lax.rem(z, 2) == 0, 2, -2)

    def pieces(i):
        got = []
        for back in (3, 2, 1):
            chunk = z - back
            live = chunk >= 0
            got_up, got_down, _, _, _ = route(jnp.maximum(chunk, 0))
            src = jnp.where(i == 0, z, source(got_up, got_down, i))
            got.append((jnp.where(live, chunk, z), jnp.where(live, src, z), live))
        step = jnp.where(i == 1, -1, 0)
        for at, value in ((2, 1), (3, near), (4, 4), (5, 3), (6, -3), (7, -near)):
            step = jnp.where(i == at, value, step)
        got.append(w_piece(step))
        return got

    def ready(half, got):
        for n, (chunk, src, live) in enumerate(got):
            piece = chunk * 8 + src
            at = slice(n * PIECE, (n + 1) * PIECE)
            vt[half, 0:D, at] = kv[piece, :, :, D : 2 * D].reshape(PIECE, D).T
            seen = in_doc(spread(lax.broadcasted_iota(jnp.int32, (PIECE, D), 0)), chunk * 2048 + src * 256)
            lanes = lax.broadcasted_iota(jnp.int32, (PIECE, D), 1)
            flag = jnp.where(live, jnp.where(seen, 1.0, 0.0), jnp.where(lanes == 16, 1.0, 0.0))
            kd[half, at, :] = flag.astype(BF)

    turn = [lax.rem(y + 1 + j, 4) for j in range(4)]

    def block(r):
        return pl.ds(pl.multiple_of(r * ROWS, ROWS), ROWS)

    def score(half, got, r, slot):
        q = q_aug[block(r), :]
        best = None
        for n, (chunk, src, *_) in enumerate(got):
            at = slice(n * PIECE, (n + 1) * PIECE)
            k = kv[chunk * 8 + src, :, :, 0:D].reshape(PIECE, D)
            k = jnp.concatenate([k, kd[half, at, :]], axis=1)
            s = lax.dot_general(k, q, (((1,), (1,)), ((), ())), preferred_element_type=F32)
            if n == 4:
                key = spread(lax.broadcasted_iota(jnp.int32, (PIECE, ROWS), 0))
                query = r * 64 + (lax.broadcasted_iota(jnp.int32, (PIECE, ROWS), 1) & 63)
                s = jnp.where(key <= query, s, HIDE)
            sb[slot, at, :] = s
            here = jnp.max(s, axis=0, keepdims=True)
            best = here if best is None else jnp.maximum(best, here)
        mb[slot, 0:1, :] = best

    def mix(half, count, r, slot):
        cols = block(r)
        old = top[0:1, cols]
        new = jnp.maximum(old, mb[slot, 0:1, :])
        shift = new * SCALE
        sums = acc[:, cols] * jnp.exp2((old - new) * SCALE)
        for n in range(count):
            at = slice(n * PIECE, (n + 1) * PIECE)
            w = jnp.exp2(sb[slot, at, :] * SCALE - shift).astype(BF)
            sums = sums + jnp.dot(vt[half, :, at], w, preferred_element_type=F32)
        acc[:, cols] = sums
        top[0:1, cols] = new

    chain_first(True)
    own_q.wait()
    build(y)
    for d in (1, 3, 2):
        q_wait(d)
        build(lax.rem(y + 4 - d, 4))
    chain(1, True)
    across_first(True)
    from_twin_first()
    start = pieces(jnp.int32(0))
    ready(0, start)
    score(0, start, turn[0], 0)

    def step(i, carry):
        half = lax.rem(i, 2)
        now = pieces(i)
        score(half, now, turn[1], 1)
        mix(half, 4, turn[0], 0)
        score(half, now, turn[2], 0)
        mix(half, 4, turn[1], 1)
        chain(i + 2, True)
        across(i + 1, True)
        score(half, now, turn[3], 1)
        mix(half, 4, turn[2], 0)
        from_twin(i + 1)
        later = pieces(i + 1)
        ready(1 - half, later)
        score(1 - half, later, turn[0], 0)
        mix(half, 4, turn[3], 1)
        return carry

    lax.fori_loop(0, 6, step, 0)

    now = pieces(jnp.int32(6))
    end = pieces(jnp.int32(7)) + [(z, rank, z >= 0)]
    ready(1, end)

    def o_copy(d):
        who = lax.rem(y + d, 4)
        return pltpu.make_async_remote_copy(
            src_ref=o_send.at[who],
            dst_ref=cut(out, y, G * D),
            send_sem=o_ssem.at[d - 1],
            recv_sem=o_rsem.at[d - 1],
            device_id=at_y(d),
            device_id_type=MESH,
        )

    own_out = pltpu.make_async_copy(o_send.at[y], cut(out, y, G * D), l_sem.at[1])
    for j in range(4):
        score(1, end, turn[j], 1)
        mix(0, 4, turn[j], 0)
        if j < 3:
            score(0, now, turn[j + 1], 0)
        mix(1, 5, turn[j], 1)
        cols = block(turn[j])
        o = (acc[0:D, cols] * (1.0 / acc[D : D + 1, cols])).T.astype(BF)
        for h in range(G):
            o_send[turn[j], :, h * D : (h + 1) * D] = o[h * 64 : (h + 1) * 64, :]
        if j < 3:
            o_copy(j + 1).start()
        else:
            own_out.start()

    k_each(False)
    for d in (1, 3, 2):
        q_copy(d).wait_send()
    chain_first(False)
    across_first(False)

    def drain(t, carry):
        chain(t, False)
        across(t, False)
        return carry

    lax.fori_loop(1, 7, drain, 0)
    for d in (1, 2, 3):
        o_copy(d).wait_send()
    for d in (1, 2, 3):
        peer = lax.rem(y + 4 - d, 4)
        pltpu.make_async_remote_copy(
            src_ref=o_send.at[peer],
            dst_ref=cut(out, peer, G * D),
            send_sem=o_ssem.at[d - 1],
            recv_sem=o_rsem.at[d - 1],
            device_id=at_y(d),
            device_id_type=MESH,
        ).wait_recv()
    own_out.wait()


def body(queries, keys, values, doc_lengths):
    anywhere = pl.BlockSpec(memory_space=pl.ANY)
    hbm = pl.BlockSpec(memory_space=pltpu.HBM)
    dma = pltpu.SemaphoreType.DMA
    return pl.pallas_call(
        kernel,
        out_shape=jax.ShapeDtypeStruct(queries.shape, BF),
        in_specs=[pl.BlockSpec(memory_space=pltpu.SMEM), hbm, hbm, hbm],
        out_specs=anywhere,
        scratch_shapes=[
            pltpu.VMEM((4, 64, G * D), BF),
            pltpu.VMEM((64, 2, PIECE // 2, 2 * D), BF),
            pltpu.VMEM((4 * ROWS, 2 * D), BF),
            pltpu.VMEM((2, 5 * PIECE, D), BF),
            pltpu.VMEM((2, VR, 5 * PIECE), BF),
            pltpu.VMEM((VR, 4 * ROWS), F32),
            pltpu.VMEM((8, 4 * ROWS), F32),
            pltpu.VMEM((2, 5 * PIECE, ROWS), F32),
            pltpu.VMEM((2, 8, ROWS), F32),
            pltpu.VMEM((4, 64, G * D), BF),
            dma((2, 2, 4)),
            dma((2, 8, 2)),
            dma((3,)),
            dma((3,)),
            dma((3, 64)),
            dma((64,)),
            dma((64,)),
            dma((64,)),
            dma((64,)),
            dma((3,)),
            dma((3,)),
            dma((2,)),
        ],
        compiler_params=pltpu.CompilerParams(
            collective_id=0, has_side_effects=True, vmem_limit_bytes=60 * 2**20
        ),
        cost_estimate=pl.CostEstimate(
            flops=12 * 10**9, bytes_accessed=10**7, transcendentals=18 * 10**6
        ),
    )(doc_lengths, queries, keys, values)


def solution(mesh):
    return jax.shard_map(
        body,
        mesh=mesh,
        in_specs=(P(("row", "col"), None), P(("col", "row"), None), P(("col", "row"), None), P()),
        out_specs=P(("row", "col"), None),
        check_vma=False,
    )
```

```python
import jax
import jax.numpy as jnp
from jax import lax
from jax.experimental import pallas as pl
from jax.experimental.pallas import tpu as pltpu
from jax.sharding import PartitionSpec as P

D = 128
G = 8
BF = jnp.bfloat16
F32 = jnp.float32
LOG2E = 1.4426950408889634
SCALE = LOG2E / D**0.5
HIDE = -1e30
FLOOR = -3e30
PIECE = 256
ROWS = 512
VR = 144
MESH = pl.DeviceIdType.MESH


def kernel(
    lengths,
    queries,
    keys,
    values,
    out,
    q_in,
    q_out,
    k_out,
    kv,
    q_aug,
    kd,
    vt,
    acc,
    top,
    sb,
    mb,
    o_send,
    k_send,
    k_recv,
    q_send,
    q_recv,
    c_send,
    c_recv,
    x_recv,
    t_send,
    t_recv,
    o_ssem,
    o_rsem,
    l_sem,
    s_sem,
):
    row = lax.axis_index("row")
    col = lax.axis_index("col")
    z = row // 4
    x_hi = (row // 2) % 2
    core = row % 2
    x_lo = col // 4
    y = col % 4
    x = x_hi * 2 + x_lo
    rank = x_hi * 4 + core * 2 + x_lo
    first = z * 2048 + rank * 256
    up = (lax.rem(row + 4, 32), col)
    down = (lax.rem(row + 28, 32), col)
    twin = (row + 1 - 2 * core, col)

    def at_y(d):
        return (row, x_lo * 4 + lax.rem(y + d, 4))

    def at_x(d, k):
        xd = lax.rem(x + d, 4)
        return (z * 4 + (xd // 2) * 2 + k, (xd % 2) * 4 + y)

    selfish = (lax.rem(y, 2) == core) & (core == x_lo)

    barrier = pltpu.get_barrier_semaphore()

    def greet(who):
        pl.semaphore_signal(barrier, inc=1, device_id=who, device_id_type=MESH)

    for who in (twin, up, down, at_x(1, core), at_x(3, core), at_y(1), at_y(2), at_y(3)):
        greet(who)
    for j in range(4):
        chunk = core + 2 * j
        for n in range(2):
            who = (z * 4 + n * 2 + x_lo, chunk)

            @pl.when(jnp.logical_not(selfish & (n == x_hi) & (chunk == col)))
            def _():
                greet(who)

    def cut(ref, head, width):
        return ref.at[:, pl.ds(pl.multiple_of(head * width, width), width)]

    def slot(chunk, half, who):
        rows = pl.ds(pl.multiple_of(who * 64, 64), 64)
        return kv.at[chunk * 8 + z, half, rows, :]

    def k_copy(n, d):
        head = lax.rem(y + d, 4)
        return pltpu.make_async_remote_copy(
            src_ref=k_out.at[head],
            dst_ref=slot(col, core, x_hi),
            send_sem=k_send.at[n, d],
            recv_sem=k_recv.at[col, x_hi],
            device_id=(z * 4 + n * 2 + lax.rem(y, 2), core * 4 + head),
            device_id_type=MESH,
        )

    def k_local():
        return pltpu.make_async_copy(
            k_out.at[y], slot(col, core, x_hi), k_recv.at[col, x_hi]
        )

    def k_each(act):
        for d in (1, 3, 2, 0):
            if act:
                for kind in range(2):
                    k_stage(kind, d).wait()
            for n in range(2):

                def one():
                    do(act, k_copy(n, d))

                if d == 0:
                    pl.when(jnp.logical_not(selfish & (n == x_hi)))(one)
                else:
                    one()

    def do(act, copy):
        if act:
            copy.start()
        else:
            copy.wait_send()

    def k_stage(kind, d):
        head = lax.rem(y + d, 4)
        return pltpu.make_async_copy(
            cut((keys, values)[kind], head, D),
            k_out.at[head, :, kind * D : (kind + 1) * D],
            s_sem.at[kind, d],
        )

    def q_stage(d):
        head = lax.rem(y + d, 4)
        dst = q_in.at[y] if d == 0 else q_out.at[d - 1]
        return pltpu.make_async_copy(cut(queries, head, G * D), dst, s_sem.at[2, d])

    def q_copy(d):
        return pltpu.make_async_remote_copy(
            src_ref=q_out.at[d - 1],
            dst_ref=q_in.at[y],
            send_sem=q_send.at[d - 1],
            recv_sem=q_recv.at[d - 1],
            device_id=at_y(d),
            device_id_type=MESH,
        )

    def q_wait(d):
        dst = q_in.at[lax.rem(y + 4 - d, 4)]
        pltpu.make_async_remote_copy(
            src_ref=dst,
            dst_ref=dst,
            send_sem=q_send.at[d - 1],
            recv_sem=q_recv.at[d - 1],
            device_id=at_y(d),
            device_id_type=MESH,
        ).wait_recv()

    for d in (1, 3, 2, 0):
        for kind in range(2):
            k_stage(kind, d).start()
    for d in (1, 3, 2, 0):
        q_stage(d).start()

    acc[...] = jnp.zeros_like(acc)
    top[...] = jnp.full_like(top, FLOOR)
    vt[:, D:VR, :] = jnp.ones((2, VR - D, 5 * PIECE), BF)

    lane = lax.broadcasted_iota(jnp.int32, (1, D), 1)
    doc_first = jnp.zeros((1, D), jnp.int32)
    doc_end = jnp.zeros((1, D), jnp.int32)
    total = jnp.int32(0)
    for d in range(16):
        doc_first = jnp.where(lane == d, total, doc_first)
        total = total + lengths[d]
        doc_end = jnp.where(lane == d, total, doc_end)

    def in_doc(offsets, start):
        pos = start + offsets
        return (pos >= doc_first) & (pos < doc_end)

    def spread(i):
        return (i & 63) + ((i >> 6) & 1) * 128 + ((i >> 7) & 1) * 64

    pl.semaphore_wait(barrier, 16 - jnp.where(selfish, 1, 0))
    k_each(True)

    @pl.when(selfish)
    def _():
        k_local().start()

    for d in (1, 3, 2):
        q_stage(d).wait()
        q_copy(d).start()

    def build(b):
        offsets = lax.broadcasted_iota(jnp.int32, (64, D), 0)
        seen = in_doc(offsets, first + b * 64)
        lanes = lax.broadcasted_iota(jnp.int32, (64, D), 1)
        wall = jnp.where(lanes < 16, jnp.where(seen, 0.0, HIDE), jnp.where(lanes == 16, HIDE, 0.0))
        wall = wall.astype(BF)
        for h in range(G):
            at = pl.ds(pl.multiple_of((b * G + h) * 64, 64), 64)
            q_aug[at, 0:D] = q_in[b, :, h * D : (h + 1) * D]
            q_aug[at, D : 2 * D] = wall

    def route(chunk):
        last = jnp.minimum(chunk + 4, 7)
        before = 1 + lax.rem(chunk, 2)
        behind = jnp.maximum(chunk, 3) - before
        most_up = before + last - chunk
        most_down = behind + last - chunk
        u = lax.rem(z - chunk + before + 16, 8)
        v = lax.rem(last + behind - z + 16, 8)
        in_up = u <= most_up
        in_down = v <= most_down
        got_up = jnp.where(in_up, u, 0)
        got_down = jnp.where(in_down, v, 0)
        on_up = in_up & (u < most_up)
        on_down = in_down & (v < most_down)
        wanted = (z >= chunk) & (z <= chunk + 4)
        return got_up, got_down, on_up, on_down, wanted

    def source(got_up, got_down, i):
        both = jnp.minimum(got_up, got_down)
        paired = i <= 2 * both
        step = jnp.where(paired, (i + 1) // 2, i - both)
        rising = jnp.where(paired, lax.rem(i, 2) == 1, got_up > got_down)
        return lax.rem(jnp.where(rising, z - step, z + step) + 8, 8)

    mine = [(core + 2 * j, route(core + 2 * j)) for j in range(4)]
    theirs = [(1 - core + 2 * j, route(1 - core + 2 * j)) for j in range(4)]

    def c_copy(way, piece, side=0):
        who = (up, down, at_x(1 + 2 * side, core))[way]
        return pltpu.make_async_remote_copy(
            src_ref=kv.at[piece, x_lo],
            dst_ref=kv.at[piece, x_lo],
            send_sem=c_send.at[way, piece],
            recv_sem=c_recv.at[piece],
            device_id=who,
            device_id_type=MESH,
        )

    def x_arrival(piece):
        return pltpu.make_async_remote_copy(
            src_ref=kv.at[piece, 1 - x_lo],
            dst_ref=kv.at[piece, 1 - x_lo],
            send_sem=c_send.at[2, piece],
            recv_sem=x_recv.at[piece],
            device_id=up,
            device_id_type=MESH,
        )

    def x_copy(piece, side):
        return pltpu.make_async_remote_copy(
            src_ref=kv.at[piece, x_lo],
            dst_ref=kv.at[piece, x_lo],
            send_sem=c_send.at[2, piece],
            recv_sem=x_recv.at[piece],
            device_id=at_x(1 + 2 * side, core),
            device_id_type=MESH,
        )

    def t_copy(piece):
        return pltpu.make_async_remote_copy(
            src_ref=kv.at[piece],
            dst_ref=kv.at[piece],
            send_sem=t_send.at[piece],
            recv_sem=t_recv.at[piece],
            device_id=twin,
            device_id_type=MESH,
        )

    def spread_x(act, chunk, src):
        do(act, x_copy(chunk * 8 + src, lax.rem(chunk // 2 + src, 2)))

    def sides(t, got_up, got_down):
        return (
            (t <= got_up, lax.rem(z - t + 8, 8)),
            (t <= got_down, lax.rem(z + t, 8)),
        )

    def chain_first(act):
        for chunk, (_, _, on_up, on_down, wanted) in mine:
            if act:
                for who in range(2):
                    pltpu.make_async_copy(
                        k_out.at[0], slot(chunk, x_lo, who), k_recv.at[chunk, who]
                    ).wait()
            piece = chunk * 8 + z

            @pl.when(wanted)
            def _():
                spread_x(act, chunk, z)

            @pl.when(on_up)
            def _():
                do(act, c_copy(0, piece))

            @pl.when(on_down)
            def _():
                do(act, c_copy(1, piece))

    def chain(t, act, part=slice(0, 4)):
        for chunk, (got_up, got_down, on_up, on_down, wanted) in mine[part]:
            for way, (there, src) in enumerate(sides(t, got_up, got_down)):

                @pl.when(there)
                def _():
                    piece = chunk * 8 + src
                    if act:
                        c_copy(way, piece).wait_recv()

                    @pl.when((on_up, on_down)[way])
                    def _():
                        do(act, c_copy(way, piece))

                    @pl.when(wanted)
                    def _():
                        spread_x(act, chunk, src)

    def across(t, act, part=slice(0, 4)):
        for chunk, (got_up, got_down, _, _, wanted) in mine[part]:
            for there, src in sides(t, got_up, got_down):

                @pl.when(there & wanted)
                def _():
                    piece = chunk * 8 + src
                    if act:
                        x_arrival(piece).wait_recv()
                    do(act, t_copy(piece))

    def across_first(act):
        for chunk, route_of in mine:

            @pl.when(route_of[4])
            def _():
                piece = chunk * 8 + z
                if act:
                    x_arrival(piece).wait_recv()
                do(act, t_copy(piece))

    def from_twin(t):
        for chunk, (got_up, got_down, _, _, wanted) in theirs:
            for there, src in sides(t, got_up, got_down):

                @pl.when(there & wanted)
                def _():
                    t_copy(chunk * 8 + src).wait_recv()

    def from_twin_first():
        for chunk, route_of in theirs:

            @pl.when(route_of[4])
            def _():
                t_copy(chunk * 8 + z).wait_recv()

    def w_piece(step):
        src = lax.rem(z + step + 8, 8)
        chunk = jnp.where(src < rank, z, z - 4)
        live = chunk >= 0
        return jnp.where(live, chunk, z), jnp.where(live, src, z), live

    near = jnp.where(lax.rem(z, 2) == 0, 2, -2)

    def pieces(i):
        got = []
        for back in (3, 2, 1):
            chunk = z - back
            live = chunk >= 0
            got_up, got_down, _, _, _ = route(jnp.maximum(chunk, 0))
            src = jnp.where(i == 0, z, source(got_up, got_down, i))
            got.append((jnp.where(live, chunk, z), jnp.where(live, src, z), live))
        step = jnp.where(i == 1, -1, 0)
        for at, value in ((2, 1), (3, near), (4, 4), (5, 3), (6, -3), (7, -near)):
            step = jnp.where(i == at, value, step)
        got.append(w_piece(step))
        return got

    def ready(half, got):
        for n, (chunk, src, live) in enumerate(got):
            piece = chunk * 8 + src
            at = slice(n * PIECE, (n + 1) * PIECE)
            vt[half, 0:D, at] = kv[piece, :, :, D : 2 * D].reshape(PIECE, D).T
            seen = in_doc(spread(lax.broadcasted_iota(jnp.int32, (PIECE, D), 0)), chunk * 2048 + src * 256)
            lanes = lax.broadcasted_iota(jnp.int32, (PIECE, D), 1)
            flag = jnp.where(live, jnp.where(seen, 1.0, 0.0), jnp.where(lanes == 16, 1.0, 0.0))
            kd[half, at, :] = flag.astype(BF)

    turn = [lax.rem(y + 1 + j, 4) for j in range(4)]

    def block(r):
        return pl.ds(pl.multiple_of(r * ROWS, ROWS), ROWS)

    def score(half, got, r, slot):
        q = q_aug[block(r), :]
        best = None
        for n, (chunk, src, *_) in enumerate(got):
            at = slice(n * PIECE, (n + 1) * PIECE)
            k = kv[chunk * 8 + src, :, :, 0:D].reshape(PIECE, D)
            k = jnp.concatenate([k, kd[half, at, :]], axis=1)
            s = lax.dot_general(k, q, (((1,), (1,)), ((), ())), preferred_element_type=F32)
            if n == 4:
                key = spread(lax.broadcasted_iota(jnp.int32, (PIECE, ROWS), 0))
                query = r * 64 + (lax.broadcasted_iota(jnp.int32, (PIECE, ROWS), 1) & 63)
                s = jnp.where(key <= query, s, HIDE)
            sb[slot, at, :] = s
            here = jnp.max(s, axis=0, keepdims=True)
            best = here if best is None else jnp.maximum(best, here)
        mb[slot, 0:1, :] = best

    def mix(half, count, r, slot):
        cols = block(r)
        old = top[0:1, cols]
        new = jnp.maximum(old, mb[slot, 0:1, :])
        shift = new * SCALE
        sums = acc[:, cols] * jnp.exp2((old - new) * SCALE)
        for n in range(count):
            at = slice(n * PIECE, (n + 1) * PIECE)
            w = jnp.exp2(sb[slot, at, :] * SCALE - shift).astype(BF)
            sums = sums + jnp.dot(vt[half, :, at], w, preferred_element_type=F32)
        acc[:, cols] = sums
        top[0:1, cols] = new

    chain_first(True)
    q_stage(0).wait()
    build(y)
    chain(1, True)
    across_first(True)

    def build_next(d, carry):
        build(lax.rem(y + d, 4))
        return carry

    for d in (1, 3, 2):
        q_wait(d)
    lax.fori_loop(1, 4, build_next, 0)
    from_twin_first()
    start = pieces(jnp.int32(0))
    ready(0, start)
    score(0, start, turn[0], 0)

    def step(i, carry):
        half = lax.rem(i, 2)
        now = pieces(i)
        chain(i + 2, True, slice(0, 2))
        across(i + 1, True, slice(0, 2))
        score(half, now, turn[1], 1)
        mix(half, 4, turn[0], 0)
        chain(i + 2, True, slice(2, 4))
        across(i + 1, True, slice(2, 4))
        score(half, now, turn[2], 0)
        mix(half, 4, turn[1], 1)
        score(half, now, turn[3], 1)
        mix(half, 4, turn[2], 0)
        from_twin(i + 1)
        later = pieces(i + 1)
        ready(1 - half, later)
        score(1 - half, later, turn[0], 0)
        mix(half, 4, turn[3], 1)
        return carry

    lax.fori_loop(0, 6, step, 0)

    now = pieces(jnp.int32(6))
    end = pieces(jnp.int32(7)) + [(z, rank, z >= 0)]
    ready(1, end)

    def o_copy(d):
        who = lax.rem(y + d, 4)
        return pltpu.make_async_remote_copy(
            src_ref=o_send.at[who],
            dst_ref=cut(out, y, G * D),
            send_sem=o_ssem.at[d - 1],
            recv_sem=o_rsem.at[d - 1],
            device_id=at_y(d),
            device_id_type=MESH,
        )

    own_out = pltpu.make_async_copy(o_send.at[y], cut(out, y, G * D), l_sem.at[0])
    for j in range(4):
        score(1, end, turn[j], 1)
        mix(0, 4, turn[j], 0)
        if j < 3:
            score(0, now, turn[j + 1], 0)
        mix(1, 5, turn[j], 1)
        cols = block(turn[j])
        o = (acc[0:D, cols] * (1.0 / acc[D : D + 1, cols])).T.astype(BF)
        for h in range(G):
            o_send[turn[j], :, h * D : (h + 1) * D] = o[h * 64 : (h + 1) * 64, :]
        if j < 3:
            o_copy(j + 1).start()
        else:
            own_out.start()

    k_each(False)
    for d in (1, 3, 2):
        q_copy(d).wait_send()
    chain_first(False)
    across_first(False)

    def drain(t, carry):
        chain(t, False)
        across(t, False)
        return carry

    lax.fori_loop(1, 7, drain, 0)
    for d in (1, 2, 3):
        o_copy(d).wait_send()
    for d in (1, 2, 3):
        peer = lax.rem(y + 4 - d, 4)
        pltpu.make_async_remote_copy(
            src_ref=o_send.at[peer],
            dst_ref=cut(out, peer, G * D),
            send_sem=o_ssem.at[d - 1],
            recv_sem=o_rsem.at[d - 1],
            device_id=at_y(d),
            device_id_type=MESH,
        ).wait_recv()
    own_out.wait()


def body(queries, keys, values, doc_lengths):
    anywhere = pl.BlockSpec(memory_space=pl.ANY)
    hbm = pl.BlockSpec(memory_space=pltpu.HBM)
    dma = pltpu.SemaphoreType.DMA
    return pl.pallas_call(
        kernel,
        out_shape=jax.ShapeDtypeStruct(queries.shape, BF),
        in_specs=[pl.BlockSpec(memory_space=pltpu.SMEM), hbm, hbm, hbm],
        out_specs=anywhere,
        scratch_shapes=[
            pltpu.VMEM((4, 64, G * D), BF),
            pltpu.VMEM((3, 64, G * D), BF),
            pltpu.VMEM((4, 64, 2 * D), BF),
            pltpu.VMEM((64, 2, PIECE // 2, 2 * D), BF),
            pltpu.VMEM((4 * ROWS, 2 * D), BF),
            pltpu.VMEM((2, 5 * PIECE, D), BF),
            pltpu.VMEM((2, VR, 5 * PIECE), BF),
            pltpu.VMEM((VR, 4 * ROWS), F32),
            pltpu.VMEM((8, 4 * ROWS), F32),
            pltpu.VMEM((2, 5 * PIECE, ROWS), F32),
            pltpu.VMEM((2, 8, ROWS), F32),
            pltpu.VMEM((4, 64, G * D), BF),
            dma((2, 4)),
            dma((8, 2)),
            dma((3,)),
            dma((3,)),
            dma((3, 64)),
            dma((64,)),
            dma((64,)),
            dma((64,)),
            dma((64,)),
            dma((3,)),
            dma((3,)),
            dma((1,)),
            dma((3, 4)),
        ],
        compiler_params=pltpu.CompilerParams(
            collective_id=0, has_side_effects=True, vmem_limit_bytes=60 * 2**20
        ),
        cost_estimate=pl.CostEstimate(
            flops=12 * 10**9, bytes_accessed=10**7, transcendentals=18 * 10**6
        ),
    )(doc_lengths, queries, keys, values)


def solution(mesh):
    return jax.shard_map(
        body,
        mesh=mesh,
        in_specs=(P(("row", "col"), None), P(("col", "row"), None), P(("col", "row"), None), P()),
        out_specs=P(("row", "col"), None),
        check_vma=False,
    )
```

```python
import jax
import jax.numpy as jnp
from jax import lax
from jax.experimental import pallas as pl
from jax.experimental.pallas import tpu as pltpu
from jax.sharding import PartitionSpec as P

D = 128
G = 8
BF = jnp.bfloat16
F32 = jnp.float32
LOG2E = 1.4426950408889634
SCALE = LOG2E / D**0.5
HIDE = -1e30
FLOOR = -3e30
PIECE = 256
ROWS = 512
VR = 144
MESH = pl.DeviceIdType.MESH


def kernel(
    lengths,
    queries,
    keys,
    values,
    out,
    q_in,
    q_out,
    k_out,
    kv,
    q_aug,
    kd,
    vt,
    acc,
    top,
    sb,
    mb,
    o_send,
    k_send,
    k_recv,
    q_send,
    q_recv,
    c_send,
    c_recv,
    x_recv,
    t_send,
    t_recv,
    o_ssem,
    o_rsem,
    l_sem,
    s_sem,
):
    row = lax.axis_index("row")
    col = lax.axis_index("col")
    z = row // 4
    x_hi = (row // 2) % 2
    core = row % 2
    x_lo = col // 4
    y = col % 4
    x = x_hi * 2 + x_lo
    rank = x_hi * 4 + core * 2 + x_lo
    first = z * 2048 + rank * 256
    up = (lax.rem(row + 4, 32), col)
    down = (lax.rem(row + 28, 32), col)
    twin = (row + 1 - 2 * core, col)

    def at_y(d):
        return (row, x_lo * 4 + lax.rem(y + d, 4))

    def at_x(d, k):
        xd = lax.rem(x + d, 4)
        return (z * 4 + (xd // 2) * 2 + k, (xd % 2) * 4 + y)

    selfish = (lax.rem(y, 2) == core) & (core == x_lo)

    barrier = pltpu.get_barrier_semaphore()

    def greet(who):
        pl.semaphore_signal(barrier, inc=1, device_id=who, device_id_type=MESH)

    for who in (twin, up, down, at_x(1, core), at_x(3, core), at_y(1), at_y(2), at_y(3)):
        greet(who)
    for j in range(4):
        chunk = core + 2 * j
        for n in range(2):
            who = (z * 4 + n * 2 + x_lo, chunk)

            @pl.when(jnp.logical_not(selfish & (n == x_hi) & (chunk == col)))
            def _():
                greet(who)

    def cut(ref, head, width):
        return ref.at[:, pl.ds(pl.multiple_of(head * width, width), width)]

    def slot(chunk, half, who):
        rows = pl.ds(pl.multiple_of(who * 64, 64), 64)
        return kv.at[chunk * 8 + z, half, rows, :]

    def k_copy(n, d):
        head = lax.rem(y + d, 4)
        return pltpu.make_async_remote_copy(
            src_ref=k_out.at[head],
            dst_ref=slot(col, core, x_hi),
            send_sem=k_send.at[n, d],
            recv_sem=k_recv.at[col, x_hi],
            device_id=(z * 4 + n * 2 + lax.rem(y, 2), core * 4 + head),
            device_id_type=MESH,
        )

    def k_local():
        return pltpu.make_async_copy(
            k_out.at[y], slot(col, core, x_hi), k_recv.at[col, x_hi]
        )

    def k_each(act):
        for d in (1, 3, 2, 0):
            if act:
                for kind in range(2):
                    k_stage(kind, d).wait()
            for n in range(2):

                def one():
                    do(act, k_copy(n, d))

                if d == 0:
                    pl.when(jnp.logical_not(selfish & (n == x_hi)))(one)
                else:
                    one()

    def do(act, copy):
        if act:
            copy.start()
        else:
            copy.wait_send()

    def k_stage(kind, d):
        head = lax.rem(y + d, 4)
        return pltpu.make_async_copy(
            cut((keys, values)[kind], head, D),
            k_out.at[head, :, kind * D : (kind + 1) * D],
            s_sem.at[kind, d],
        )

    def q_stage(d):
        head = lax.rem(y + d, 4)
        dst = q_in.at[y] if d == 0 else q_out.at[d - 1]
        return pltpu.make_async_copy(cut(queries, head, G * D), dst, s_sem.at[2, d])

    def q_copy(d):
        return pltpu.make_async_remote_copy(
            src_ref=q_out.at[d - 1],
            dst_ref=q_in.at[y],
            send_sem=q_send.at[d - 1],
            recv_sem=q_recv.at[d - 1],
            device_id=at_y(d),
            device_id_type=MESH,
        )

    def q_wait(d):
        dst = q_in.at[lax.rem(y + 4 - d, 4)]
        pltpu.make_async_remote_copy(
            src_ref=dst,
            dst_ref=dst,
            send_sem=q_send.at[d - 1],
            recv_sem=q_recv.at[d - 1],
            device_id=at_y(d),
            device_id_type=MESH,
        ).wait_recv()

    for d in (1, 3, 2, 0):
        for kind in range(2):
            k_stage(kind, d).start()
    for d in (1, 3, 2, 0):
        q_stage(d).start()

    acc[...] = jnp.zeros_like(acc)
    top[...] = jnp.full_like(top, FLOOR)
    vt[:, D:VR, :] = jnp.ones((2, VR - D, 5 * PIECE), BF)

    lane = lax.broadcasted_iota(jnp.int32, (1, D), 1)
    doc_first = jnp.zeros((1, D), jnp.int32)
    doc_end = jnp.zeros((1, D), jnp.int32)
    total = jnp.int32(0)
    for d in range(16):
        doc_first = jnp.where(lane == d, total, doc_first)
        total = total + lengths[d]
        doc_end = jnp.where(lane == d, total, doc_end)

    def in_doc(offsets, start):
        pos = start + offsets
        return (pos >= doc_first) & (pos < doc_end)

    def spread(i):
        return (i & 63) + ((i >> 6) & 1) * 128 + ((i >> 7) & 1) * 64

    pl.semaphore_wait(barrier, 16 - jnp.where(selfish, 1, 0))
    k_each(True)

    @pl.when(selfish)
    def _():
        k_local().start()

    for d in (1, 3, 2):
        q_stage(d).wait()
        q_copy(d).start()

    def build(b):
        offsets = lax.broadcasted_iota(jnp.int32, (64, D), 0)
        seen = in_doc(offsets, first + b * 64)
        lanes = lax.broadcasted_iota(jnp.int32, (64, D), 1)
        wall = jnp.where(lanes < 16, jnp.where(seen, 0.0, HIDE), jnp.where(lanes == 16, HIDE, 0.0))
        wall = wall.astype(BF)
        for h in range(G):
            at = pl.ds(pl.multiple_of((b * G + h) * 64, 64), 64)
            q_aug[at, 0:D] = q_in[b, :, h * D : (h + 1) * D]
            q_aug[at, D : 2 * D] = wall

    def route(chunk):
        last = jnp.minimum(chunk + 4, 7)
        before = 1 + lax.rem(chunk, 2)
        behind = jnp.maximum(chunk, 3) - before
        most_up = before + last - chunk
        most_down = behind + last - chunk
        u = lax.rem(z - chunk + before + 16, 8)
        v = lax.rem(last + behind - z + 16, 8)
        in_up = u <= most_up
        in_down = v <= most_down
        got_up = jnp.where(in_up, u, 0)
        got_down = jnp.where(in_down, v, 0)
        on_up = in_up & (u < most_up)
        on_down = in_down & (v < most_down)
        wanted = (z >= chunk) & (z <= chunk + 4)
        return got_up, got_down, on_up, on_down, wanted

    def source(got_up, got_down, i):
        both = jnp.minimum(got_up, got_down)
        paired = i <= 2 * both
        step = jnp.where(paired, (i + 1) // 2, i - both)
        rising = jnp.where(paired, lax.rem(i, 2) == 1, got_up > got_down)
        return lax.rem(jnp.where(rising, z - step, z + step) + 8, 8)

    mine = [(core + 2 * j, route(core + 2 * j)) for j in range(4)]
    theirs = [(1 - core + 2 * j, route(1 - core + 2 * j)) for j in range(4)]

    def c_copy(way, piece, side=0):
        who = (up, down, at_x(1 + 2 * side, core))[way]
        return pltpu.make_async_remote_copy(
            src_ref=kv.at[piece, x_lo],
            dst_ref=kv.at[piece, x_lo],
            send_sem=c_send.at[way, piece],
            recv_sem=c_recv.at[piece],
            device_id=who,
            device_id_type=MESH,
        )

    def x_arrival(piece):
        return pltpu.make_async_remote_copy(
            src_ref=kv.at[piece, 1 - x_lo],
            dst_ref=kv.at[piece, 1 - x_lo],
            send_sem=c_send.at[2, piece],
            recv_sem=x_recv.at[piece],
            device_id=up,
            device_id_type=MESH,
        )

    def x_copy(piece, side):
        return pltpu.make_async_remote_copy(
            src_ref=kv.at[piece, x_lo],
            dst_ref=kv.at[piece, x_lo],
            send_sem=c_send.at[2, piece],
            recv_sem=x_recv.at[piece],
            device_id=at_x(1 + 2 * side, core),
            device_id_type=MESH,
        )

    def t_copy(piece):
        return pltpu.make_async_remote_copy(
            src_ref=kv.at[piece],
            dst_ref=kv.at[piece],
            send_sem=t_send.at[piece],
            recv_sem=t_recv.at[piece],
            device_id=twin,
            device_id_type=MESH,
        )

    def spread_x(act, chunk, src):
        do(act, x_copy(chunk * 8 + src, lax.rem(chunk // 2 + src, 2)))

    def sides(t, got_up, got_down):
        return (
            (t <= got_up, lax.rem(z - t + 8, 8)),
            (t <= got_down, lax.rem(z + t, 8)),
        )

    def chain_first(act):
        for chunk, (_, _, on_up, on_down, wanted) in mine:
            if act:
                for who in range(2):
                    pltpu.make_async_copy(
                        k_out.at[0], slot(chunk, x_lo, who), k_recv.at[chunk, who]
                    ).wait()
            piece = chunk * 8 + z

            @pl.when(wanted)
            def _():
                spread_x(act, chunk, z)

            @pl.when(on_up)
            def _():
                do(act, c_copy(0, piece))

            @pl.when(on_down)
            def _():
                do(act, c_copy(1, piece))

    def chain(t, act, part=slice(0, 4)):
        for chunk, (got_up, got_down, on_up, on_down, wanted) in mine[part]:
            for way, (there, src) in enumerate(sides(t, got_up, got_down)):

                @pl.when(there)
                def _():
                    piece = chunk * 8 + src
                    if act:
                        c_copy(way, piece).wait_recv()

                    @pl.when((on_up, on_down)[way])
                    def _():
                        do(act, c_copy(way, piece))

                    @pl.when(wanted)
                    def _():
                        spread_x(act, chunk, src)

    def across(t, act, part=slice(0, 4)):
        for chunk, (got_up, got_down, _, _, wanted) in mine[part]:
            for there, src in sides(t, got_up, got_down):

                @pl.when(there & wanted)
                def _():
                    piece = chunk * 8 + src
                    if act:
                        x_arrival(piece).wait_recv()
                    do(act, t_copy(piece))

    def across_first(act):
        for chunk, route_of in mine:

            @pl.when(route_of[4])
            def _():
                piece = chunk * 8 + z
                if act:
                    x_arrival(piece).wait_recv()
                do(act, t_copy(piece))

    def from_twin(t):
        for chunk, (got_up, got_down, _, _, wanted) in theirs:
            for there, src in sides(t, got_up, got_down):

                @pl.when(there & wanted)
                def _():
                    t_copy(chunk * 8 + src).wait_recv()

    def from_twin_first():
        for chunk, route_of in theirs:

            @pl.when(route_of[4])
            def _():
                t_copy(chunk * 8 + z).wait_recv()

    def w_piece(step):
        src = lax.rem(z + step + 8, 8)
        chunk = jnp.where(src < rank, z, z - 4)
        live = chunk >= 0
        return jnp.where(live, chunk, z), jnp.where(live, src, z), live

    near = jnp.where(lax.rem(z, 2) == 0, 2, -2)

    def pieces(i):
        got = []
        for back in (3, 2, 1):
            chunk = z - back
            live = chunk >= 0
            got_up, got_down, _, _, _ = route(jnp.maximum(chunk, 0))
            src = jnp.where(i == 0, z, source(got_up, got_down, i))
            got.append((jnp.where(live, chunk, z), jnp.where(live, src, z), live))
        step = jnp.where(i == 1, -1, 0)
        for at, value in ((2, 1), (3, near), (4, 4), (5, 3), (6, -3), (7, -near)):
            step = jnp.where(i == at, value, step)
        got.append(w_piece(step))
        return got

    def ready(half, got):
        for n, (chunk, src, live) in enumerate(got):
            piece = chunk * 8 + src
            at = slice(n * PIECE, (n + 1) * PIECE)
            vt[half, 0:D, at] = kv[piece, :, :, D : 2 * D].reshape(PIECE, D).T
            seen = in_doc(spread(lax.broadcasted_iota(jnp.int32, (PIECE, D), 0)), chunk * 2048 + src * 256)
            lanes = lax.broadcasted_iota(jnp.int32, (PIECE, D), 1)
            flag = jnp.where(live, jnp.where(seen, 1.0, 0.0), jnp.where(lanes == 16, 1.0, 0.0))
            kd[half, at, :] = flag.astype(BF)

    turn = [lax.rem(y + 1 + j, 4) for j in range(4)]

    def block(r):
        return pl.ds(pl.multiple_of(r * ROWS, ROWS), ROWS)

    def score(half, got, r, slot):
        q = q_aug[block(r), :]
        best = None
        for n, (chunk, src, *_) in enumerate(got):
            at = slice(n * PIECE, (n + 1) * PIECE)
            k = kv[chunk * 8 + src, :, :, 0:D].reshape(PIECE, D)
            k = jnp.concatenate([k, kd[half, at, :]], axis=1)
            s = lax.dot_general(k, q, (((1,), (1,)), ((), ())), preferred_element_type=F32)
            if n == 4:
                key = spread(lax.broadcasted_iota(jnp.int32, (PIECE, ROWS), 0))
                query = r * 64 + (lax.broadcasted_iota(jnp.int32, (PIECE, ROWS), 1) & 63)
                s = jnp.where(key <= query, s, HIDE)
            sb[slot, at, :] = s
            here = jnp.max(s, axis=0, keepdims=True)
            best = here if best is None else jnp.maximum(best, here)
        mb[slot, 0:1, :] = best

    def mix(half, count, r, slot):
        cols = block(r)
        old = top[0:1, cols]
        new = jnp.maximum(old, mb[slot, 0:1, :])
        shift = new * SCALE
        sums = acc[:, cols] * jnp.exp2((old - new) * SCALE)
        for n in range(count):
            at = slice(n * PIECE, (n + 1) * PIECE)
            w = jnp.exp2(sb[slot, at, :] * SCALE - shift).astype(BF)
            sums = sums + jnp.dot(vt[half, :, at], w, preferred_element_type=F32)
        acc[:, cols] = sums
        top[0:1, cols] = new

    chain_first(True)
    q_stage(0).wait()
    build(y)
    chain(1, True)
    across_first(True)

    def build_next(d, carry):
        build(lax.rem(y + d, 4))
        return carry

    for d in (1, 3, 2):
        q_wait(d)
    lax.fori_loop(1, 4, build_next, 0)
    from_twin_first()
    start = pieces(jnp.int32(0))
    ready(0, start)
    score(0, start, turn[0], 0)

    def step(i, carry):
        half = lax.rem(i, 2)
        now = pieces(i)
        chain(i + 2, True, slice(0, 2))
        across(i + 1, True, slice(0, 2))
        score(half, now, turn[1], 1)
        mix(half, 4, turn[0], 0)
        chain(i + 2, True, slice(2, 4))
        across(i + 1, True, slice(2, 4))
        score(half, now, turn[2], 0)
        mix(half, 4, turn[1], 1)
        score(half, now, turn[3], 1)
        mix(half, 4, turn[2], 0)
        from_twin(i + 1)
        later = pieces(i + 1)
        ready(1 - half, later)
        score(1 - half, later, turn[0], 0)
        mix(half, 4, turn[3], 1)
        return carry

    lax.fori_loop(0, 6, step, 0)

    now = pieces(jnp.int32(6))
    end = pieces(jnp.int32(7)) + [(z, rank, z >= 0)]
    ready(1, end)

    def o_copy(d):
        who = lax.rem(y + d, 4)
        return pltpu.make_async_remote_copy(
            src_ref=o_send.at[who],
            dst_ref=cut(out, y, G * D),
            send_sem=o_ssem.at[d - 1],
            recv_sem=o_rsem.at[d - 1],
            device_id=at_y(d),
            device_id_type=MESH,
        )

    own_out = pltpu.make_async_copy(o_send.at[y], cut(out, y, G * D), l_sem.at[0])
    for j in range(4):
        score(1, end, turn[j], 1)
        mix(0, 4, turn[j], 0)
        if j < 3:
            score(0, now, turn[j + 1], 0)
        mix(1, 5, turn[j], 1)
        cols = block(turn[j])
        o = (acc[0:D, cols] * (1.0 / acc[D : D + 1, cols])).T.astype(BF)
        for h in range(G):
            o_send[turn[j], :, h * D : (h + 1) * D] = o[h * 64 : (h + 1) * 64, :]
        if j < 3:
            o_copy(j + 1).start()
        else:
            own_out.start()

    k_each(False)
    for d in (1, 3, 2):
        q_copy(d).wait_send()
    chain_first(False)
    across_first(False)

    def drain(t, carry):
        chain(t, False)
        across(t, False)
        return carry

    lax.fori_loop(1, 7, drain, 0)
    for d in (1, 2, 3):
        o_copy(d).wait_send()
    for d in (1, 2, 3):
        peer = lax.rem(y + 4 - d, 4)
        pltpu.make_async_remote_copy(
            src_ref=o_send.at[peer],
            dst_ref=cut(out, peer, G * D),
            send_sem=o_ssem.at[d - 1],
            recv_sem=o_rsem.at[d - 1],
            device_id=at_y(d),
            device_id_type=MESH,
        ).wait_recv()
    own_out.wait()


def body(queries, keys, values, doc_lengths):
    doc_lengths, queries, keys, values = (
        pltpu.with_memory_space_constraint(a, pltpu.HBM)
        for a in (doc_lengths, queries, keys, values)
    )
    anywhere = pl.BlockSpec(memory_space=pl.ANY)
    hbm = pl.BlockSpec(memory_space=pltpu.HBM)
    dma = pltpu.SemaphoreType.DMA
    return pl.pallas_call(
        kernel,
        out_shape=jax.ShapeDtypeStruct(queries.shape, BF),
        in_specs=[pl.BlockSpec(memory_space=pltpu.SMEM), hbm, hbm, hbm],
        out_specs=anywhere,
        scratch_shapes=[
            pltpu.VMEM((4, 64, G * D), BF),
            pltpu.VMEM((3, 64, G * D), BF),
            pltpu.VMEM((4, 64, 2 * D), BF),
            pltpu.VMEM((64, 2, PIECE // 2, 2 * D), BF),
            pltpu.VMEM((4 * ROWS, 2 * D), BF),
            pltpu.VMEM((2, 5 * PIECE, D), BF),
            pltpu.VMEM((2, VR, 5 * PIECE), BF),
            pltpu.VMEM((VR, 4 * ROWS), F32),
            pltpu.VMEM((8, 4 * ROWS), F32),
            pltpu.VMEM((2, 5 * PIECE, ROWS), F32),
            pltpu.VMEM((2, 8, ROWS), F32),
            pltpu.VMEM((4, 64, G * D), BF),
            dma((2, 4)),
            dma((8, 2)),
            dma((3,)),
            dma((3,)),
            dma((3, 64)),
            dma((64,)),
            dma((64,)),
            dma((64,)),
            dma((64,)),
            dma((3,)),
            dma((3,)),
            dma((1,)),
            dma((3, 4)),
        ],
        compiler_params=pltpu.CompilerParams(
            collective_id=0, has_side_effects=True, vmem_limit_bytes=40 * 2**20
        ),
        cost_estimate=pl.CostEstimate(
            flops=12 * 10**9, bytes_accessed=10**7, transcendentals=18 * 10**6
        ),
    )(doc_lengths, queries, keys, values)


def solution(mesh):
    return jax.shard_map(
        body,
        mesh=mesh,
        in_specs=(P(("row", "col"), None), P(("col", "row"), None), P(("col", "row"), None), P()),
        out_specs=P(("row", "col"), None),
        check_vma=False,
    )
```

```python
import jax
import jax.numpy as jnp
from jax import lax
from jax.experimental import pallas as pl
from jax.experimental.pallas import tpu as pltpu
from jax.sharding import PartitionSpec as P

D = 128
G = 8
BF = jnp.bfloat16
F32 = jnp.float32
LOG2E = 1.4426950408889634
SCALE = LOG2E / D**0.5
HIDE = -1e30
FLOOR = -3e30
PIECE = 256
ROWS = 512
VR = 144
MESH = pl.DeviceIdType.MESH


def kernel(
    lengths,
    queries,
    keys,
    values,
    out,
    q_in,
    q_out,
    k_out,
    kv,
    q_aug,
    kd,
    vt,
    acc,
    top,
    sb,
    mb,
    o_send,
    k_send,
    k_recv,
    q_send,
    q_recv,
    c_send,
    c_recv,
    x_recv,
    t_send,
    t_recv,
    o_ssem,
    o_rsem,
    l_sem,
    s_sem,
):
    row = lax.axis_index("row")
    col = lax.axis_index("col")
    z = row // 4
    x_hi = (row // 2) % 2
    core = row % 2
    x_lo = col // 4
    y = col % 4
    x = x_hi * 2 + x_lo
    rank = x_hi * 4 + core * 2 + x_lo
    first = z * 2048 + rank * 256
    up = (lax.rem(row + 4, 32), col)
    down = (lax.rem(row + 28, 32), col)
    twin = (row + 1 - 2 * core, col)

    def at_y(d):
        return (row, x_lo * 4 + lax.rem(y + d, 4))

    def at_x(d, k):
        xd = lax.rem(x + d, 4)
        return (z * 4 + (xd // 2) * 2 + k, (xd % 2) * 4 + y)

    selfish = (lax.rem(y, 2) == core) & (core == x_lo)

    barrier = pltpu.get_barrier_semaphore()

    def greet(who):
        pl.semaphore_signal(barrier, inc=1, device_id=who, device_id_type=MESH)

    for who in (twin, up, down, at_x(1, core), at_x(3, core), at_y(1), at_y(2), at_y(3)):
        greet(who)
    for j in range(4):
        chunk = core + 2 * j
        for n in range(2):
            who = (z * 4 + n * 2 + x_lo, chunk)

            @pl.when(jnp.logical_not(selfish & (n == x_hi) & (chunk == col)))
            def _():
                greet(who)

    def cut(ref, head, width):
        return ref.at[:, pl.ds(pl.multiple_of(head * width, width), width)]

    def slot(chunk, half, who):
        rows = pl.ds(pl.multiple_of(who * 64, 64), 64)
        return kv.at[chunk * 8 + z, half, rows, :]

    def k_copy(n, d):
        head = lax.rem(y + d, 4)
        return pltpu.make_async_remote_copy(
            src_ref=k_out.at[head],
            dst_ref=slot(col, core, x_hi),
            send_sem=k_send.at[n, d],
            recv_sem=k_recv.at[col, x_hi],
            device_id=(z * 4 + n * 2 + lax.rem(y, 2), core * 4 + head),
            device_id_type=MESH,
        )

    def k_local():
        return pltpu.make_async_copy(
            k_out.at[y], slot(col, core, x_hi), k_recv.at[col, x_hi]
        )

    def k_each(act):
        for d in (1, 3, 2, 0):
            if act:
                for kind in range(2):
                    k_stage(kind, d).wait()
            for n in range(2):

                def one():
                    do(act, k_copy(n, d))

                if d == 0:
                    pl.when(jnp.logical_not(selfish & (n == x_hi)))(one)
                else:
                    one()

    def do(act, copy):
        if act:
            copy.start()
        else:
            copy.wait_send()

    def k_stage(kind, d):
        head = lax.rem(y + d, 4)
        return pltpu.make_async_copy(
            cut((keys, values)[kind], head, D),
            k_out.at[head, :, kind * D : (kind + 1) * D],
            s_sem.at[kind, d],
        )

    def q_stage(d):
        head = lax.rem(y + d, 4)
        dst = q_in.at[y] if d == 0 else q_out.at[d - 1]
        return pltpu.make_async_copy(cut(queries, head, G * D), dst, s_sem.at[2, d])

    def q_copy(d):
        return pltpu.make_async_remote_copy(
            src_ref=q_out.at[d - 1],
            dst_ref=q_in.at[y],
            send_sem=q_send.at[d - 1],
            recv_sem=q_recv.at[d - 1],
            device_id=at_y(d),
            device_id_type=MESH,
        )

    def q_wait(d):
        dst = q_in.at[lax.rem(y + 4 - d, 4)]
        pltpu.make_async_remote_copy(
            src_ref=dst,
            dst_ref=dst,
            send_sem=q_send.at[d - 1],
            recv_sem=q_recv.at[d - 1],
            device_id=at_y(d),
            device_id_type=MESH,
        ).wait_recv()

    for d in (1, 3, 2, 0):
        for kind in range(2):
            k_stage(kind, d).start()
    for d in (1, 3, 2, 0):
        q_stage(d).start()

    acc[...] = jnp.zeros_like(acc)
    top[...] = jnp.full_like(top, FLOOR)
    vt[:, D:VR, :] = jnp.ones((2, VR - D, 5 * PIECE), BF)

    lane = lax.broadcasted_iota(jnp.int32, (1, D), 1)
    doc_first = jnp.zeros((1, D), jnp.int32)
    doc_end = jnp.zeros((1, D), jnp.int32)
    total = jnp.int32(0)
    for d in range(16):
        doc_first = jnp.where(lane == d, total, doc_first)
        total = total + lengths[d]
        doc_end = jnp.where(lane == d, total, doc_end)

    def in_doc(offsets, start):
        pos = start + offsets
        return (pos >= doc_first) & (pos < doc_end)

    def spread(i):
        return (i & 63) + ((i >> 6) & 1) * 128 + ((i >> 7) & 1) * 64

    pl.semaphore_wait(barrier, 16 - jnp.where(selfish, 1, 0))
    k_each(True)

    @pl.when(selfish)
    def _():
        k_local().start()

    for d in (1, 3, 2):
        q_stage(d).wait()
        q_copy(d).start()

    def build(b):
        offsets = lax.broadcasted_iota(jnp.int32, (64, D), 0)
        seen = in_doc(offsets, first + b * 64)
        lanes = lax.broadcasted_iota(jnp.int32, (64, D), 1)
        wall = jnp.where(lanes < 16, jnp.where(seen, 0.0, HIDE), jnp.where(lanes == 16, HIDE, 0.0))
        wall = wall.astype(BF)
        for h in range(G):
            at = pl.ds(pl.multiple_of((b * G + h) * 64, 64), 64)
            q_aug[at, 0:D] = q_in[b, :, h * D : (h + 1) * D]
            q_aug[at, D : 2 * D] = wall

    def route(chunk):
        last = jnp.minimum(chunk + 4, 7)
        before = 1 + lax.rem(chunk, 2)
        behind = jnp.maximum(chunk, 3) - before
        most_up = before + last - chunk
        most_down = behind + last - chunk
        u = lax.rem(z - chunk + before + 16, 8)
        v = lax.rem(last + behind - z + 16, 8)
        in_up = u <= most_up
        in_down = v <= most_down
        got_up = jnp.where(in_up, u, 0)
        got_down = jnp.where(in_down, v, 0)
        on_up = in_up & (u < most_up)
        on_down = in_down & (v < most_down)
        wanted = (z >= chunk) & (z <= chunk + 4)
        return got_up, got_down, on_up, on_down, wanted

    def source(got_up, got_down, i):
        both = jnp.minimum(got_up, got_down)
        paired = i <= 2 * both
        step = jnp.where(paired, (i + 1) // 2, i - both)
        rising = jnp.where(paired, lax.rem(i, 2) == 1, got_up > got_down)
        return lax.rem(jnp.where(rising, z - step, z + step) + 8, 8)

    mine = [(core + 2 * j, route(core + 2 * j)) for j in range(4)]
    theirs = [(1 - core + 2 * j, route(1 - core + 2 * j)) for j in range(4)]

    def c_copy(way, piece, side=0):
        who = (up, down, at_x(1 + 2 * side, core))[way]
        return pltpu.make_async_remote_copy(
            src_ref=kv.at[piece, x_lo],
            dst_ref=kv.at[piece, x_lo],
            send_sem=c_send.at[way, piece],
            recv_sem=c_recv.at[piece],
            device_id=who,
            device_id_type=MESH,
        )

    def x_arrival(piece):
        return pltpu.make_async_remote_copy(
            src_ref=kv.at[piece, 1 - x_lo],
            dst_ref=kv.at[piece, 1 - x_lo],
            send_sem=c_send.at[2, piece],
            recv_sem=x_recv.at[piece],
            device_id=up,
            device_id_type=MESH,
        )

    def x_copy(piece, side):
        return pltpu.make_async_remote_copy(
            src_ref=kv.at[piece, x_lo],
            dst_ref=kv.at[piece, x_lo],
            send_sem=c_send.at[2, piece],
            recv_sem=x_recv.at[piece],
            device_id=at_x(1 + 2 * side, core),
            device_id_type=MESH,
        )

    def t_copy(piece):
        return pltpu.make_async_remote_copy(
            src_ref=kv.at[piece],
            dst_ref=kv.at[piece],
            send_sem=t_send.at[piece],
            recv_sem=t_recv.at[piece],
            device_id=twin,
            device_id_type=MESH,
        )

    def spread_x(act, chunk, src):
        do(act, x_copy(chunk * 8 + src, lax.rem(chunk // 2 + src, 2)))

    def sides(t, got_up, got_down):
        return (
            (t <= got_up, lax.rem(z - t + 8, 8)),
            (t <= got_down, lax.rem(z + t, 8)),
        )

    def chain_first(act):
        for chunk, (_, _, on_up, on_down, wanted) in mine:
            if act:
                for who in range(2):
                    pltpu.make_async_copy(
                        k_out.at[0], slot(chunk, x_lo, who), k_recv.at[chunk, who]
                    ).wait()
            piece = chunk * 8 + z

            @pl.when(wanted)
            def _():
                spread_x(act, chunk, z)

            @pl.when(on_up)
            def _():
                do(act, c_copy(0, piece))

            @pl.when(on_down)
            def _():
                do(act, c_copy(1, piece))

    def chain(t, act, part=slice(0, 4)):
        for chunk, (got_up, got_down, on_up, on_down, wanted) in mine[part]:
            for way, (there, src) in enumerate(sides(t, got_up, got_down)):

                @pl.when(there)
                def _():
                    piece = chunk * 8 + src
                    if act:
                        c_copy(way, piece).wait_recv()

                    @pl.when((on_up, on_down)[way])
                    def _():
                        do(act, c_copy(way, piece))

                    @pl.when(wanted)
                    def _():
                        spread_x(act, chunk, src)

    def across(t, act, part=slice(0, 4)):
        for chunk, (got_up, got_down, _, _, wanted) in mine[part]:
            for there, src in sides(t, got_up, got_down):

                @pl.when(there & wanted)
                def _():
                    piece = chunk * 8 + src
                    if act:
                        x_arrival(piece).wait_recv()
                    do(act, t_copy(piece))

    def across_first(act):
        for chunk, route_of in mine:

            @pl.when(route_of[4])
            def _():
                piece = chunk * 8 + z
                if act:
                    x_arrival(piece).wait_recv()
                do(act, t_copy(piece))

    def from_twin(t):
        for chunk, (got_up, got_down, _, _, wanted) in theirs:
            for there, src in sides(t, got_up, got_down):

                @pl.when(there & wanted)
                def _():
                    t_copy(chunk * 8 + src).wait_recv()

    def from_twin_first():
        for chunk, route_of in theirs:

            @pl.when(route_of[4])
            def _():
                t_copy(chunk * 8 + z).wait_recv()

    def w_piece(step):
        src = lax.rem(z + step + 8, 8)
        chunk = jnp.where(src < rank, z, z - 4)
        live = chunk >= 0
        return jnp.where(live, chunk, z), jnp.where(live, src, z), live

    near = jnp.where(lax.rem(z, 2) == 0, 2, -2)

    def pieces(i):
        got = []
        for back in (3, 2, 1):
            chunk = z - back
            live = chunk >= 0
            got_up, got_down, _, _, _ = route(jnp.maximum(chunk, 0))
            src = jnp.where(i == 0, z, source(got_up, got_down, i))
            got.append((jnp.where(live, chunk, z), jnp.where(live, src, z), live))
        step = jnp.where(i == 1, -1, 0)
        for at, value in ((2, 1), (3, near), (4, 4), (5, 3), (6, -3), (7, -near)):
            step = jnp.where(i == at, value, step)
        got.append(w_piece(step))
        return got

    def ready(half, got):
        for n, (chunk, src, live) in enumerate(got):
            piece = chunk * 8 + src
            at = slice(n * PIECE, (n + 1) * PIECE)
            vt[half, 0:D, at] = kv[piece, :, :, D : 2 * D].reshape(PIECE, D).T
            seen = in_doc(spread(lax.broadcasted_iota(jnp.int32, (PIECE, D), 0)), chunk * 2048 + src * 256)
            lanes = lax.broadcasted_iota(jnp.int32, (PIECE, D), 1)
            flag = jnp.where(live, jnp.where(seen, 1.0, 0.0), jnp.where(lanes == 16, 1.0, 0.0))
            kd[half, at, 0:D] = kv[piece, :, :, 0:D].reshape(PIECE, D)
            kd[half, at, D : 2 * D] = flag.astype(BF)

    turn = [lax.rem(y + 1 + j, 4) for j in range(4)]

    def block(r):
        return pl.ds(pl.multiple_of(r * ROWS, ROWS), ROWS)

    def score(half, got, r, slot):
        q = q_aug[block(r), :]
        wide = 4 * PIECE
        s = lax.dot_general(
            kd[half, 0:wide, :], q, (((1,), (1,)), ((), ())), preferred_element_type=F32
        )
        sb[slot, 0:wide, :] = s
        best = jnp.max(s, axis=0, keepdims=True)
        if len(got) == 5:
            at = slice(wide, wide + PIECE)
            s = lax.dot_general(
                kd[half, at, :], q, (((1,), (1,)), ((), ())), preferred_element_type=F32
            )
            key = spread(lax.broadcasted_iota(jnp.int32, (PIECE, ROWS), 0))
            query = r * 64 + (lax.broadcasted_iota(jnp.int32, (PIECE, ROWS), 1) & 63)
            s = jnp.where(key <= query, s, HIDE)
            sb[slot, at, :] = s
            best = jnp.maximum(best, jnp.max(s, axis=0, keepdims=True))
        mb[slot, 0:1, :] = best

    def mix(half, count, r, slot):
        cols = block(r)
        old = top[0:1, cols]
        new = jnp.maximum(old, mb[slot, 0:1, :])
        at = slice(0, count * PIECE)
        w = jnp.exp2(sb[slot, at, :] * SCALE - new * SCALE).astype(BF)
        sums = acc[:, cols] * jnp.exp2((old - new) * SCALE)
        acc[:, cols] = sums + jnp.dot(vt[half, :, at], w, preferred_element_type=F32)
        top[0:1, cols] = new

    chain_first(True)
    q_stage(0).wait()
    build(y)
    chain(1, True)
    across_first(True)

    def build_next(d, carry):
        build(lax.rem(y + d, 4))
        return carry

    for d in (1, 3, 2):
        q_wait(d)
    lax.fori_loop(1, 4, build_next, 0)
    from_twin_first()
    start = pieces(jnp.int32(0))
    ready(0, start)
    score(0, start, turn[0], 0)

    def step(i, carry):
        half = lax.rem(i, 2)
        now = pieces(i)
        chain(i + 2, True, slice(0, 2))
        across(i + 1, True, slice(0, 2))
        score(half, now, turn[1], 1)
        mix(half, 4, turn[0], 0)
        chain(i + 2, True, slice(2, 4))
        across(i + 1, True, slice(2, 4))
        score(half, now, turn[2], 0)
        mix(half, 4, turn[1], 1)
        score(half, now, turn[3], 1)
        mix(half, 4, turn[2], 0)
        from_twin(i + 1)
        later = pieces(i + 1)
        ready(1 - half, later)
        score(1 - half, later, turn[0], 0)
        mix(half, 4, turn[3], 1)
        return carry

    lax.fori_loop(0, 6, step, 0)

    now = pieces(jnp.int32(6))
    end = pieces(jnp.int32(7)) + [(z, rank, z >= 0)]
    ready(1, end)

    def o_copy(d):
        who = lax.rem(y + d, 4)
        return pltpu.make_async_remote_copy(
            src_ref=o_send.at[who],
            dst_ref=cut(out, y, G * D),
            send_sem=o_ssem.at[d - 1],
            recv_sem=o_rsem.at[d - 1],
            device_id=at_y(d),
            device_id_type=MESH,
        )

    own_out = pltpu.make_async_copy(o_send.at[y], cut(out, y, G * D), l_sem.at[0])
    for j in range(4):
        score(1, end, turn[j], 1)
        mix(0, 4, turn[j], 0)
        if j < 3:
            score(0, now, turn[j + 1], 0)
        mix(1, 5, turn[j], 1)
        cols = block(turn[j])
        o = (acc[0:D, cols] * (1.0 / acc[D : D + 1, cols])).T.astype(BF)
        for h in range(G):
            o_send[turn[j], :, h * D : (h + 1) * D] = o[h * 64 : (h + 1) * 64, :]
        if j < 3:
            o_copy(j + 1).start()
        else:
            own_out.start()

    k_each(False)
    for d in (1, 3, 2):
        q_copy(d).wait_send()
    chain_first(False)
    across_first(False)

    def drain(t, carry):
        chain(t, False)
        across(t, False)
        return carry

    lax.fori_loop(1, 7, drain, 0)
    for d in (1, 2, 3):
        o_copy(d).wait_send()
    for d in (1, 2, 3):
        peer = lax.rem(y + 4 - d, 4)
        pltpu.make_async_remote_copy(
            src_ref=o_send.at[peer],
            dst_ref=cut(out, peer, G * D),
            send_sem=o_ssem.at[d - 1],
            recv_sem=o_rsem.at[d - 1],
            device_id=at_y(d),
            device_id_type=MESH,
        ).wait_recv()
    own_out.wait()


def body(queries, keys, values, doc_lengths):
    doc_lengths, queries, keys, values = (
        pltpu.with_memory_space_constraint(a, pltpu.HBM)
        for a in (doc_lengths, queries, keys, values)
    )
    anywhere = pl.BlockSpec(memory_space=pl.ANY)
    hbm = pl.BlockSpec(memory_space=pltpu.HBM)
    dma = pltpu.SemaphoreType.DMA
    return pl.pallas_call(
        kernel,
        out_shape=jax.ShapeDtypeStruct(queries.shape, BF),
        in_specs=[pl.BlockSpec(memory_space=pltpu.SMEM), hbm, hbm, hbm],
        out_specs=anywhere,
        scratch_shapes=[
            pltpu.VMEM((4, 64, G * D), BF),
            pltpu.VMEM((3, 64, G * D), BF),
            pltpu.VMEM((4, 64, 2 * D), BF),
            pltpu.VMEM((64, 2, PIECE // 2, 2 * D), BF),
            pltpu.VMEM((4 * ROWS, 2 * D), BF),
            pltpu.VMEM((2, 5 * PIECE, 2 * D), BF),
            pltpu.VMEM((2, VR, 5 * PIECE), BF),
            pltpu.VMEM((VR, 4 * ROWS), F32),
            pltpu.VMEM((8, 4 * ROWS), F32),
            pltpu.VMEM((2, 5 * PIECE, ROWS), F32),
            pltpu.VMEM((2, 8, ROWS), F32),
            pltpu.VMEM((4, 64, G * D), BF),
            dma((2, 4)),
            dma((8, 2)),
            dma((3,)),
            dma((3,)),
            dma((3, 64)),
            dma((64,)),
            dma((64,)),
            dma((64,)),
            dma((64,)),
            dma((3,)),
            dma((3,)),
            dma((1,)),
            dma((3, 4)),
        ],
        compiler_params=pltpu.CompilerParams(
            collective_id=0, has_side_effects=True, vmem_limit_bytes=40 * 2**20
        ),
        cost_estimate=pl.CostEstimate(
            flops=12 * 10**9, bytes_accessed=10**7, transcendentals=18 * 10**6
        ),
    )(doc_lengths, queries, keys, values)


def solution(mesh):
    return jax.shard_map(
        body,
        mesh=mesh,
        in_specs=(P(("row", "col"), None), P(("col", "row"), None), P(("col", "row"), None), P()),
        out_specs=P(("row", "col"), None),
        check_vma=False,
    )
```
